512 devices in a mesh: seq: 64 (over z, x), head: 2 (over core), dp: 4 (over y).
Axes of the slice: x: 4, y: 4, z: 16, core: 2. Of those that a mesh axis runs over, the one named last changes fastest.
Arguments:
- hidden: bfloat16 [4, 12288, 1024], P('dp', 'seq'), may hold values from -6 to 6
- norm_gain: float32 [1024], replicated, may hold values from 0.5 to 1.5
- projection: bfloat16 [3, 1024, 1024], P(None, None, 'head'), may hold values from -1 to 1
- upstream: bfloat16 [4, 12288, 1024], P('dp', 'seq', 'head'), may hold values from -6 to 6
- cluster: int32 [4, 12288, 1], P('dp', 'seq'), may hold values from 0 to 63; in each aligned block of 192 rows (0 to 191, 192 to 383, ..., all dimensions but the last counted through in order) at most 9 rows name the same one
Outputs:
- input_gradient: bfloat16 [4, 12288, 1024], P('dp', 'seq', 'head')
- gain_gradient: float32 [1024], P('head')
The draws below stay inside these ranges and needn't reach their ends.
Inputs may be any that keep to these rules, and one draw needn't show every extreme that they name: Among the 192 tokens of one device no cluster is named more than 9 times, a bound that some block reaches.
All inputs are finite; a program needn't handle non-finite values.
Results may differ from the reference program's by a relative error of at most 0.01.
The reference program's roundings to bfloat16 on the way count: a program that leaves them out, or rounds other values in their place, can miss the bound.
Values may be sent and summed in bfloat16 or wider, within the bound.
No kernel may reach another device: no remote copies, remote signals or barrier semaphores. Data moves between devices by JAX's collectives and lax.ppermute only.
A program may use at most 64 MiB of HBM per device.

```python
import math
import jax
import jax.numpy as jnp
import numpy as np
from jax import lax

D = 1024
HDIM = 64
TOK_DEV = 192
CLUSTERS = 64
HE = 1024
GROUP_HEADS = 8
LEN = 12288
SEQS = 4
SLOT = 9
ROWS = 576
N_HEAD = 2


def draw_hidden(key, part):
    samples = jax.random.normal(jax.random.fold_in(key, 1), (SEQS, LEN, D), jnp.float32)
    return jnp.clip(samples, -6.0, 6.0).astype(jnp.bfloat16)


def draw_projection(key, part):
    weights_base = jax.random.normal(jax.random.fold_in(key, 11), (3, D, HE), jnp.float32) / math.sqrt(D)
    return jnp.clip(weights_base, -1.0, 1.0).astype(jnp.bfloat16)


def levels(stream_key, shape, shards, low, top_value):
    def one(axis_at, blocks):
        steps = jax.random.uniform(jax.random.fold_in(jax.random.fold_in(stream_key, 6), axis_at), (blocks,), jnp.float32, low / len(shards), top_value / len(shards))
        return jnp.repeat(jnp.exp(steps), shape[axis_at] // blocks).reshape((-1,) + (1,) * (len(shape) - axis_at - 1))

    loudness = one(*shards[0])
    for cut in shards[1:]:
        loudness = loudness * one(*cut)
    return loudness


def deal_out(stream_key, own, number, rows, count, top, reach, skew):
    ranking = jax.random.permutation(stream_key, count)
    heavy_load, ordinary = portions_of(count, rows * top, reach, skew, True), portions_of(count, rows * top, reach, skew, False)
    places = jnp.arange(count)

    def named(lengths, offset_by):
        used = int((lengths > 0).sum())
        fixed = max(1, used // 4)
        passed = fixed + (places - fixed + offset_by * (used - fixed)) % max(1, count - fixed)
        return jnp.zeros((count,), jnp.int32).at[ranking[jnp.where(places < fixed, places, passed)]].set(jnp.asarray(lengths, jnp.int32))

    lengths = jnp.where(number % 4 == 0, named(heavy_load, number // 4), named(ordinary, number - number // 4 - 1))
    mixed = jax.random.permutation(jax.random.fold_in(own, 3), count)
    source_of, taker = mixed[0:count // 2 * 2:2], mixed[1:count // 2 * 2:2]
    room = jnp.minimum(lengths[source_of] - 1, reach - lengths[taker]) // 2
    room = jnp.where((source_of == ranking[0]) | (taker == ranking[0]) | (lengths[taker] == 0), 0, jnp.maximum(room, 0))
    passed = jax.random.randint(jax.random.fold_in(own, 4), (count // 2,), 0, 1 << 20) % (room + 1)
    lengths = lengths.at[source_of].add(-passed).at[taker].add(passed)
    items = jnp.searchsorted(jnp.cumsum(lengths), jnp.arange(rows * top), side="right").astype(jnp.int32)
    listing = items.reshape(top, rows).T
    listing = listing[jax.random.permutation(jax.random.fold_in(own, 1), rows)]
    offset_by = jax.random.randint(jax.random.fold_in(own, 2), (rows, 1), 0, top)
    return jnp.take_along_axis(listing, (jnp.arange(top)[None, :] + offset_by) % top, axis=1)


def portions_of(number_of, total, bound, skew, full):
    loads = [(1 << 20) // math.isqrt(grade ** skew) + 1 for grade in range(1, number_of + 1)]
    largest = bound if full else min(bound, max(-(-total // number_of), total * loads[0] // sum(loads)))
    least = 1 if total - largest >= number_of - 1 else 0
    given, spare = [largest] + [least] * (number_of - 1), total - largest - least * (number_of - 1)
    while spare > 0:
        free = [i for i in range(1, number_of) if given[i] < largest] or [i for i in range(1, number_of) if given[i] < bound]
        whole, left = sum([loads[i] for i in free]), spare
        for i in free:
            extra = min(bound - given[i], max(1, left * loads[i] // whole), spare)
            given[i] = given[i] + extra
            spare = spare - extra
    return np.array(given)


def gaussian(own_key, shape, deviation, most, split=(), held_as=jnp.bfloat16):
    drawn = deviation * jax.random.normal(own_key, shape, jnp.float32)
    if split:
        drawn = drawn * levels(own_key, shape, split, -0.22, 0.18)
    return jnp.clip(drawn, -most, most).astype(held_as)


def setup_inputs(seed: int = 0) -> dict:
    splits = jax.random.split(jax.random.key(seed), 6)
    hidden = draw_hidden(jax.random.fold_in(splits[5], 71), 0)
    norm_gain = jnp.clip(1.0 + 0.1 * jax.random.normal(splits[1], (D,), jnp.float32), 0.5, 1.5)
    projection = draw_projection(jax.random.fold_in(splits[5], 71), 0)
    upstream = gaussian(splits[3], (SEQS, LEN, HE), 1.0, 6.0, ((0, 4), (1, 64), (2, 2)))
    cluster_keys = jax.random.split(jax.random.fold_in(splits[4], 1), SEQS * LEN // TOK_DEV)
    cluster_turns = jax.random.permutation(jax.random.fold_in(splits[4], 3), SEQS * LEN // TOK_DEV)
    cluster = jax.vmap(lambda own, number: deal_out(jax.random.fold_in(splits[4], 2), own, number, TOK_DEV, CLUSTERS, 1, SLOT, 2))(cluster_keys, cluster_turns).reshape((SEQS, LEN, 1))
    return dict(hidden=hidden, norm_gain=norm_gain, projection=projection, upstream=upstream, cluster=cluster)


epsilon = 1e-05
masked = -1e+30

def normalize(values, norm_gain):
    values = values.astype(jnp.float32)
    center = values - lax.optimization_barrier(jnp.mean(values, -1, keepdims=True))
    spread = lax.rsqrt(lax.optimization_barrier(jnp.mean(center * center, -1, keepdims=True)) + epsilon)
    scaled = center * spread
    return (scaled, spread, (scaled * norm_gain).astype(jnp.bfloat16))

def attend_backward(queries, key_rows, values, upstream, allowed, factor):
    scores = lax.dot_general(queries, key_rows, (((1,), (1,)), ((), ())), preferred_element_type=jnp.float32) * factor
    scores = jnp.where(allowed, scores, masked)
    powers = jnp.exp(scores - lax.optimization_barrier(jnp.max(scores, -1, keepdims=True)))
    weights = powers / lax.optimization_barrier(jnp.sum(powers, -1, keepdims=True))
    rounded = weights.astype(jnp.bfloat16)
    output = jnp.dot(rounded, values, preferred_element_type=jnp.float32)
    center_term = lax.optimization_barrier(jnp.sum(upstream.astype(jnp.float32) * output, -1, keepdims=True))
    grad_values = lax.dot_general(rounded, upstream, (((0,), (0,)), ((), ())), preferred_element_type=jnp.float32).astype(jnp.bfloat16)
    grad_weights = lax.dot_general(upstream, values, (((1,), (1,)), ((), ())), preferred_element_type=jnp.float32)
    grad_scores = (weights * (grad_weights - center_term) * factor).astype(jnp.bfloat16)
    grad_queries = jnp.dot(grad_scores, key_rows, preferred_element_type=jnp.float32).astype(jnp.bfloat16)
    grad_keys = lax.dot_general(grad_scores, queries, (((0,), (0,)), ((), ())), preferred_element_type=jnp.float32).astype(jnp.bfloat16)
    return (grad_queries, grad_keys, grad_values)

def cluster_grads(payload, validity, head_width):
    row_count = payload.shape[0]
    spans = payload.shape[1] // 4
    heads_local = spans // head_width
    positions = lax.broadcasted_iota(jnp.int32, (row_count, row_count), 0)
    others = lax.broadcasted_iota(jnp.int32, (row_count, row_count), 1)
    allowed = (positions >= others) & (validity[None, :] > 0)
    factor = head_width ** (-0.5)

    def one_head(head_index, result):
        offset = head_index * head_width

        def select(portion):
            return lax.dynamic_slice_in_dim(payload, portion * spans + offset, head_width, 1)
        grads_head = attend_backward(select(0), select(1), select(2), select(3), allowed, factor)
        for portion in range(3):
            result = lax.dynamic_update_slice_in_dim(result, grads_head[portion], portion * spans + offset, 1)
        return result
    return lax.fori_loop(0, heads_local, one_head, jnp.zeros((row_count, 3 * spans), jnp.bfloat16))

def reference(hidden, norm_gain, projection, upstream, cluster):
    scaled, spread, normed = normalize(hidden, norm_gain)
    flattened = normed.reshape(-1, D)
    projected = [jnp.dot(flattened, projection[portion], preferred_element_type=jnp.float32).astype(jnp.bfloat16).reshape(SEQS, LEN, HE) for portion in range(3)]
    group_width = GROUP_HEADS * HDIM
    gradients = []
    for sequence in range(SEQS):
        labels = cluster[sequence, :, 0]
        member = (labels[:, None] == jnp.arange(CLUSTERS, dtype=jnp.int32)[None, :]).astype(jnp.int32)
        counts = lax.optimization_barrier(jnp.sum(member, 0)).astype(jnp.int32)
        ordering = jnp.argsort(labels, stable=True).astype(jnp.int32)
        starts = (jnp.cumsum(counts) - counts).astype(jnp.int32)
        within = jnp.arange(ROWS, dtype=jnp.int32)
        validity = within[None, :] < counts[:, None]
        source_rows = jnp.where(validity, ordering[jnp.minimum(starts[:, None] + within[None, :], LEN - 1)], LEN).astype(jnp.int32)
        payload = jnp.concatenate([projected[0][sequence], projected[1][sequence], projected[2][sequence], upstream[sequence]], 1)
        padded = jnp.concatenate([payload, jnp.zeros((1, 4 * HE), jnp.bfloat16)], 0)

        def per_cluster(entries):
            return cluster_grads(padded[entries[0]], entries[1].astype(jnp.float32), HDIM)
        cluster_out = lax.map(per_cluster, (source_rows, validity))
        restored = jnp.zeros((LEN + 1, 3 * HE), jnp.bfloat16).at[source_rows.reshape(-1)].set(cluster_out.reshape(-1, 3 * HE))[:LEN]
        partial_value = jnp.zeros((LEN, D), jnp.float32)
        for group_index in range(N_HEAD):
            column_start = group_index * group_width
            group_term = jnp.zeros((LEN, D), jnp.float32)
            for portion in range(3):
                first = portion * HE + column_start
                group_term = group_term + jnp.dot(restored[:, first:first + group_width], projection[portion][:, column_start:column_start + group_width].T, preferred_element_type=jnp.float32)
            partial_value = partial_value + lax.optimization_barrier(group_term.astype(jnp.bfloat16)).astype(jnp.float32)
        gradients.append(partial_value)
    grad_normed = jnp.stack(gradients, 0)
    gain_gradient = lax.optimization_barrier(jnp.sum(grad_normed * scaled, (0, 1))) * (SEQS * LEN) ** (-0.5)
    grad_scaled = grad_normed * norm_gain
    first_mean = lax.optimization_barrier(jnp.mean(grad_scaled, -1, keepdims=True))
    second_mean = lax.optimization_barrier(jnp.mean(grad_scaled * scaled, -1, keepdims=True))
    input_gradient = (spread * (grad_scaled - first_mean - scaled * second_mean)).astype(jnp.bfloat16)
    return (input_gradient, gain_gradient)
```

```python
import jax
import jax.numpy as jnp
from jax import lax
from jax.experimental import pallas as pl
from jax.experimental.pallas import tpu as pltpu
from jax.sharding import PartitionSpec as P

HDIM = 64
EPSILON = 1e-05
MASKED = -1e30
PAD_MARK = 64.0
f32 = jnp.float32
bf16 = jnp.bfloat16


def dims(lhs, rhs, left, right):
    return lax.dot_general(lhs, rhs, (((left,), (right,)), ((), ())), preferred_element_type=f32)


def iota(shape, dim):
    return lax.broadcasted_iota(jnp.int32, shape, dim)


def vmem_call(kernel, out_shape, scratch=(), limit=56, scalars=0, count=1):
    spec = pl.BlockSpec(memory_space=pltpu.VMEM)
    return pl.pallas_call(
        kernel,
        out_shape=out_shape,
        in_specs=[pl.BlockSpec(memory_space=pltpu.SMEM)] * scalars + [spec] * count,
        out_specs=jax.tree.map(lambda _: spec, out_shape),
        scratch_shapes=scratch,
        compiler_params=pltpu.CompilerParams(vmem_limit_bytes=limit * 2**20),
    )


def pack_kernel(slots, head_ref, hidden_ref, gain_ref, up_ref, lab_ref, labrow_ref, out_ref, spread_ref):
    tokens, width = hidden_ref.shape
    half = width // 2
    x = hidden_ref[...].astype(f32)
    center = x - jnp.mean(x, -1, keepdims=True)
    spread = lax.rsqrt(jnp.mean(center * center, -1, keepdims=True) + EPSILON)
    spread_ref[...] = spread
    normed = (center * spread * gain_ref[...]).astype(bf16)
    own = jnp.where(head_ref[0] == 0, normed[:, :half], normed[:, half:])
    up = up_ref[...]
    lab, labrow = lab_ref[...], labrow_ref[...]
    before = (lab == labrow) & (iota((tokens, tokens), 0) < iota((tokens, tokens), 1))
    rank = jnp.sum(before.astype(f32), 0, keepdims=True).astype(jnp.int32)
    rows = out_ref.shape[0]
    key = jnp.where(rank < slots - 1, labrow * 8 + rank, -1)
    last = jnp.where(rank == slots - 1, labrow, -1)
    row = iota((rows, tokens), 0)
    hot = (row == key).astype(f32)
    taken = jnp.sum(hot, -1, keepdims=True)
    hot = hot.astype(bf16)
    out_ref[:, :half] = dims(hot, own, 1, 0).astype(bf16)
    right = dims(hot, up, 1, 0)
    first = iota((rows, half), 1) == 0
    out_ref[:, half:width] = jnp.where(first & (taken == 0), PAD_MARK, right).astype(bf16)
    hot_last = ((row >> 3) == last).astype(f32)
    taken = jnp.sum(hot_last, -1, keepdims=True)
    piece = iota((rows, tokens), 0) & 7
    total = jnp.zeros((rows, 128), f32)
    for i in range(8):
        source = (own if i < 4 else up)[:, (i % 4) * 128 : (i % 4 + 1) * 128]
        total = total + dims(jnp.where(piece == i, hot_last, 0.0).astype(bf16), source, 1, 0)
    mark = (iota((rows, 128), 1) == 0) & ((iota((rows, 128), 0) & 7) == 4) & (taken == 0)
    out_ref[:, width:] = jnp.where(mark, PAD_MARK, total).astype(bf16)


def attend_kernel(head_ref, recv_ref, other_ref, weights_ref, gain_ref, part_ref, sums_ref,
                  x_ref, u_ref, q_ref, k_ref, v_ref, g_ref, dq_ref):
    rows, extended = recv_ref.shape
    half = weights_ref.shape[2]
    width = 2 * half
    sources = rows // 8
    total = rows + sources
    head = head_ref[0]
    pick_col, pick_row = iota((sources, rows), 1), iota((sources, rows), 0)

    def ninth(ref, i):
        pick = (pick_col == pick_row * 8 + i).astype(bf16)
        return dims(pick, ref[:, width:], 1, 0).astype(bf16)

    x_ref[0, :rows, :] = recv_ref[:, :half]
    x_ref[1, :rows, :] = other_ref[:, :half]
    u_ref[:rows, :] = recv_ref[:, half:width]
    for i in range(4):
        span = slice(i * 128, (i + 1) * 128)
        x_ref[0, rows:, span] = ninth(recv_ref, i)
        x_ref[1, rows:, span] = ninth(other_ref, i)
        u_ref[rows:, span] = ninth(recv_ref, 4 + i)
    up = u_ref[:, :128]
    pads = up[:, :1].astype(f32) > 0.5 * PAD_MARK
    u_ref[:, :128] = jnp.where(pads & (iota((total, 128), 1) == 0), 0.0, up.astype(f32)).astype(bf16)
    own_rows = pl.ds(pl.multiple_of(head * half, half), half)
    other_rows = pl.ds(pl.multiple_of((1 - head) * half, half), half)
    own, other = x_ref[0], x_ref[1]
    for n, ref in enumerate((q_ref, k_ref, v_ref)):
        ref[...] = (
            dims(own, weights_ref[n, own_rows, :], 1, 0) + dims(other, weights_ref[n, other_rows, :], 1, 0)
        ).astype(bf16)

    def order(i):
        return jnp.where(i < rows, (i >> 3) * 9 + (i & 7), (i - rows) * 9 + 8)

    factor = HDIM**-0.5
    place = jnp.where(pads, 2 * total, order(iota((total, 1), 0)))
    allowed = place <= order(iota((1, total), 1))
    left = iota((total, 128), 1) < HDIM

    def pair(p, carry):
        span = pl.ds(pl.multiple_of(p * 128, 128), 128)
        q, k, v, u = q_ref[:, span], k_ref[:, span], v_ref[:, span], u_ref[:, span]
        made = []
        for side in (left, ~left):
            ks = jnp.where(side, k, 0).astype(bf16)
            vs = jnp.where(side, v, 0).astype(bf16)
            scores = jnp.where(allowed, dims(ks, q, 1, 1) * factor, MASKED)
            powers = jnp.exp(scores - jnp.max(scores, 0, keepdims=True))
            weights = powers / jnp.sum(powers, 0, keepdims=True)
            rounded = weights.astype(bf16)
            grads = dims(vs, u, 1, 1)
            center = jnp.sum(rounded.astype(f32) * grads, 0, keepdims=True)
            ds = (weights * (grads - center) * factor).astype(bf16)
            made.append((dims(rounded, u, 1, 0), dims(ds, q, 1, 0), dims(ks, ds, 0, 0)))
        (gv0, gk0, gq0), (gv1, gk1, gq1) = made
        g_ref[0, :, span] = jnp.where(left, gk0, gk1).astype(bf16)
        g_ref[1, :, span] = jnp.where(left, gv0, gv1).astype(bf16)
        dq_ref[span, :] = (gq0 + gq1).astype(bf16)
        return carry

    lax.fori_loop(0, half // 128, pair, 0)
    for c in range(2):
        lines = slice(c * half, (c + 1) * half)
        partial = (
            dims(dq_ref[...], weights_ref[0, lines, :], 0, 1)
            + dims(g_ref[0], weights_ref[1, lines, :], 1, 1)
            + dims(g_ref[1], weights_ref[2, lines, :], 1, 1)
        ).astype(bf16)
        part_ref[:, lines] = partial
        normed = x_ref[jnp.where(head == c, 0, 1)].astype(f32)
        sums_ref[:, lines] = jnp.sum(partial.astype(f32) * normed, 0, keepdims=True) / gain_ref[:, lines]


def combine_kernel(head_ref, part_ref, other_ref, recv_ref, peer_ref, gain_ref, out_ref):
    rows = recv_ref.shape[0]
    total, width = part_ref.shape
    half = width // 2
    sources = rows // 8
    head = head_ref[0]
    pick_col, pick_row = iota((sources, rows), 1), iota((sources, rows), 0)

    def tokens_of(ref):
        pieces = [
            dims((pick_col == pick_row * 8 + i).astype(bf16), ref[:, width:], 1, 0) for i in range(4)
        ]
        return jnp.concatenate([ref[:, :half].astype(f32), jnp.concatenate(pieces, 1)], 0)

    own, peer = tokens_of(recv_ref), tokens_of(peer_ref)
    gain = gain_ref[...]

    def pick_half(array, own_half):
        return jnp.where((head == 0) == own_half, array[:, :half], array[:, half:])

    grad = part_ref[...].astype(f32) + other_ref[...].astype(f32)
    grad_own, grad_peer = pick_half(grad, True), pick_half(grad, False)
    gain_own, gain_peer = pick_half(gain, True), pick_half(gain, False)
    first = (jnp.sum(grad_own * gain_own, -1, keepdims=True) + jnp.sum(grad_peer * gain_peer, -1, keepdims=True)) / width
    second = (jnp.sum(grad_own * own, -1, keepdims=True) + jnp.sum(grad_peer * peer, -1, keepdims=True)) / width
    result = (grad_own * gain_own - first - own / gain_own * second).astype(bf16)
    out_ref[:, :half] = result[:rows]
    ext = jnp.zeros((rows, 128), f32)
    put_row, put_col = iota((rows, sources), 0), iota((rows, sources), 1)
    for i in range(4):
        put = (put_row == put_col * 8 + i).astype(bf16)
        ext = ext + dims(put, result[rows:, i * 128 : (i + 1) * 128], 1, 0)
    out_ref[:, half:] = ext.astype(bf16)


def finish_kernel(slots, back_ref, lab_ref, labrow_ref, spread_ref, out_ref):
    tokens, half = out_ref.shape
    rows = back_ref.shape[0]
    lab, labrow = lab_ref[...], labrow_ref[...]
    before = (lab == labrow) & (iota((tokens, tokens), 1) < iota((tokens, tokens), 0))
    rank = jnp.sum(before.astype(f32), -1, keepdims=True).astype(jnp.int32)
    key = jnp.where(rank < slots - 1, lab * 8 + rank, -1)
    last = jnp.where(rank == slots - 1, lab, -1)
    col = iota((tokens, rows), 1)
    hot = (col == key).astype(bf16)
    hot_last = (col >> 3) == last
    spread = spread_ref[...]
    for i in range(half // 128):
        span = slice(i * 128, (i + 1) * 128)
        value = dims(hot, back_ref[:, span], 1, 0)
        value = value + dims((hot_last & ((col & 7) == i)).astype(bf16), back_ref[:, half:], 1, 0)
        out_ref[:, span] = (value * spread).astype(bf16)


def on_device(hidden, norm_gain, projection, upstream, cluster):
    sources = lax.axis_size("seq")
    tokens, width = hidden.shape[1:]
    half = projection.shape[2]
    slots = 3 * tokens // sources
    total, rows = sources * slots, sources * 8
    head = lax.axis_index("head").astype(jnp.int32).reshape(1)
    gain = norm_gain.reshape(1, width)
    lab = cluster[0]
    labrow = lab.reshape(1, tokens)
    shape = jax.ShapeDtypeStruct
    swap = [(0, 1), (1, 0)]

    sent, spread = vmem_call(
        lambda *refs: pack_kernel(slots, *refs),
        (shape((rows, width + 128), bf16), shape((tokens, 1), f32)),
        scalars=1,
        count=5,
    )(head, hidden[0], gain, upstream[0], lab, labrow)
    recv = lax.all_to_all(sent.reshape(sources, 8, width + 128), "seq", 0, 0, tiled=True)
    recv = recv.reshape(rows, width + 128)
    peer = lax.ppermute(recv, "head", swap)
    part, sums = vmem_call(
        attend_kernel,
        (shape((total, width), bf16), shape((1, width), f32)),
        scratch=[
            pltpu.VMEM((2, total, half), bf16),
            pltpu.VMEM((total, half), bf16),
            pltpu.VMEM((total, half), bf16),
            pltpu.VMEM((total, half), bf16),
            pltpu.VMEM((total, half), bf16),
            pltpu.VMEM((2, total, half), bf16),
            pltpu.VMEM((half, total), bf16),
        ],
        scalars=1,
        count=4,
    )(head, recv, peer, projection, gain)
    other = lax.ppermute(part, "head", swap)
    answer = vmem_call(combine_kernel, shape((rows, half + 128), bf16), scalars=1, count=5)(
        head, part, other, recv, peer, gain
    )
    back = lax.all_to_all(answer.reshape(sources, 8, half + 128), "seq", 0, 0, tiled=True)
    back = back.reshape(rows, half + 128)
    side = sources // 16 if sources % 16 == 0 else 1
    across = [[z * side + x for x in range(side)] for z in range(sources // side)]
    along = [[z * side + x for z in range(sources // side)] for x in range(side)]
    gain_sum = lax.psum(sums.reshape(width), ("dp", "head"))
    gain_sum = lax.psum(gain_sum, "seq", axis_index_groups=across)
    gain_sum = lax.psum(gain_sum, "seq", axis_index_groups=along)
    gain_sum = lax.dynamic_slice_in_dim(gain_sum, head[0] * half, half, 0)
    gain_gradient = gain_sum * (sources * lax.axis_size("dp") * tokens) ** (-0.5)
    result = vmem_call(lambda *refs: finish_kernel(slots, *refs), shape((tokens, half), bf16), count=4)(
        back, lab, labrow, spread
    )
    return (result.reshape(1, tokens, half), gain_gradient)


def solution(mesh):
    in_specs = (
        P("dp", "seq", None),
        P(),
        P(None, None, "head"),
        P("dp", "seq", "head"),
        P("dp", "seq", None),
    )
    out_specs = (P("dp", "seq", "head"), P("head"))
    return jax.shard_map(
        on_device, mesh=mesh, in_specs=in_specs, out_specs=out_specs, check_vma=False
    )
```

```python
import jax
import jax.numpy as jnp
from jax import lax
from jax.experimental import pallas as pl
from jax.experimental.pallas import tpu as pltpu
from jax.sharding import PartitionSpec as P

HDIM = 64
EPSILON = 1e-05
MASKED = -1e30
PAD_MARK = 64.0
f32 = jnp.float32
bf16 = jnp.bfloat16


def dims(lhs, rhs, left, right):
    return lax.dot_general(lhs, rhs, (((left,), (right,)), ((), ())), preferred_element_type=f32)


def iota(shape, dim):
    return lax.broadcasted_iota(jnp.int32, shape, dim)


def vmem_call(kernel, out_shape, scratch=(), limit=8, scalars=0, count=1):
    spec = pl.BlockSpec(memory_space=pltpu.VMEM)
    return pl.pallas_call(
        kernel,
        out_shape=out_shape,
        in_specs=[pl.BlockSpec(memory_space=pltpu.SMEM)] * scalars + [spec] * count,
        out_specs=jax.tree.map(lambda _: spec, out_shape),
        scratch_shapes=scratch,
        compiler_params=pltpu.CompilerParams(vmem_limit_bytes=limit * 2**20),
    )


def column_of(labels):
    count = labels.shape[1]
    same = iota((count, count), 0) == iota((count, count), 1)
    return jnp.sum(jnp.where(same, labels.astype(f32), 0.0), -1, keepdims=True).astype(jnp.int32)


def pack_kernel(slots, head_ref, hidden_ref, gain_ref, up_ref, labrow_ref, out_ref, spread_ref):
    tokens, width = hidden_ref.shape
    half = width // 2
    x = hidden_ref[...].astype(f32)
    center = x - jnp.mean(x, -1, keepdims=True)
    spread = lax.rsqrt(jnp.mean(center * center, -1, keepdims=True) + EPSILON)
    spread_ref[...] = spread
    normed = (center * spread * gain_ref[...]).astype(bf16)
    own = jnp.where(head_ref[0] == 0, normed[:, :half], normed[:, half:])
    up = up_ref[...]
    labrow = labrow_ref[...]
    lab = column_of(labrow)
    before = (lab == labrow) & (iota((tokens, tokens), 0) < iota((tokens, tokens), 1))
    rank = jnp.sum(before.astype(f32), 0, keepdims=True).astype(jnp.int32)
    rows = out_ref.shape[0]
    key = jnp.where(rank < slots - 1, labrow * 8 + rank, -1)
    last = jnp.where(rank == slots - 1, labrow, -1)
    row = iota((rows, tokens), 0)
    hot = (row == key).astype(f32)
    taken = jnp.sum(hot, -1, keepdims=True)
    hot = hot.astype(bf16)
    out_ref[:, :half] = dims(hot, own, 1, 0).astype(bf16)
    right = dims(hot, up, 1, 0)
    first = iota((rows, half), 1) == 0
    out_ref[:, half:width] = jnp.where(first & (taken == 0), PAD_MARK, right).astype(bf16)
    hot_last = ((row >> 3) == last).astype(f32)
    taken = jnp.sum(hot_last, -1, keepdims=True)
    piece = iota((rows, tokens), 0) & 7
    total = jnp.zeros((rows, 128), f32)
    for i in range(8):
        source = (own if i < 4 else up)[:, (i % 4) * 128 : (i % 4 + 1) * 128]
        total = total + dims(jnp.where(piece == i, hot_last, 0.0).astype(bf16), source, 1, 0)
    mark = (iota((rows, 128), 1) == 0) & ((iota((rows, 128), 0) & 7) == 4) & (taken == 0)
    out_ref[:, width:] = jnp.where(mark, PAD_MARK, total).astype(bf16)


def thirds(value):
    high = value.astype(bf16)
    rest = value - high.astype(f32)
    middle = rest.astype(bf16)
    return high.astype(f32), middle.astype(f32), rest - middle.astype(f32)


def attend_kernel(head_ref, recv_ref, other_ref, weights_ref, gain_ref, keep_ref, send_ref, own_ref, stats_ref,
                  peer_ref, u_ref, q_ref, k_ref, v_ref, g_ref, dq_ref, bias_ref):
    rows, extended = recv_ref.shape
    half = weights_ref.shape[2]
    width = 2 * half
    late = rows // 8
    total = rows + late
    head = head_ref[0]
    pick_col, pick_row = iota((late, rows), 1), iota((late, rows), 0)
    own_ref[late:, :] = recv_ref[:, :half]
    peer_ref[late:, :] = other_ref[:, :half]
    u_ref[late:, :] = recv_ref[:, half:width]
    for i in range(4):
        span = slice(i * 128, (i + 1) * 128)
        pick = (pick_col == pick_row * 8 + i).astype(bf16)
        own_ref[:late, span] = dims(pick, recv_ref[:, width:], 1, 0).astype(bf16)
        peer_ref[:late, span] = dims(pick, other_ref[:, width:], 1, 0).astype(bf16)
        pick = (pick_col == pick_row * 8 + (i + 4)).astype(bf16)
        u_ref[:late, span] = dims(pick, recv_ref[:, width:], 1, 0).astype(bf16)
    up = u_ref[:, :128].astype(f32)
    pads = up[:, :1] > 0.5 * PAD_MARK
    u_ref[:, :128] = jnp.where(pads & (iota((total, 128), 1) == 0), 0.0, up).astype(bf16)
    own_rows = pl.ds(pl.multiple_of(head * half, half), half)
    other_rows = pl.ds(pl.multiple_of((1 - head) * half, half), half)
    own, peer = own_ref[...], peer_ref[...]
    factor = HDIM**-0.5
    for n, ref in enumerate((q_ref, k_ref, v_ref)):
        made = dims(own, weights_ref[n, own_rows, :], 1, 0) + dims(peer, weights_ref[n, other_rows, :], 1, 0)
        ref[...] = (made * factor if n == 0 else made).astype(bf16)

    def order(i):
        return jnp.where(i < late, i * 9 + 8, ((i - late) >> 3) * 9 + ((i - late) & 7))

    place = jnp.where(pads, 2 * total, order(iota((total, 1), 0)))
    column = iota((1, rows), 1) + late
    bias_ref[:, :rows] = jnp.where(place <= order(column), 0.0, MASKED)
    column = iota((1, 2 * late), 1) & (late - 1)
    bias_ref[:, rows:] = jnp.where(place <= order(column), 0.0, MASKED)
    left = iota((total, 2 * HDIM), 1) < HDIM
    block = rows // 2
    low = late + block

    def products(k, v, q, u, bias):
        return dims(k, q, 1, 1) + bias, dims(v, u, 1, 1)

    def softmax_grads(scores, grads):
        powers = jnp.exp(scores - jnp.max(scores, 0, keepdims=True))
        weights = powers * (1.0 / jnp.sum(powers, 0, keepdims=True))
        rounded = weights.astype(bf16)
        center = jnp.sum(rounded.astype(f32) * grads, 0, keepdims=True)
        return rounded, (weights * (grads - center)).astype(bf16)

    def pair(p, carry):
        start = p * 128 if isinstance(p, int) else pl.multiple_of(p * 128, 128)
        span = pl.ds(start, 128)
        q, k, v, u = q_ref[:, span], k_ref[:, span], v_ref[:, span], u_ref[:, span]
        blocks = []
        for side in (left, ~left):
            ks = jnp.where(side, k, 0).astype(bf16)
            vs = jnp.where(side, v, 0).astype(bf16)
            for reach, first in ((low, late), (total, low)):
                bias = (reach, slice(first - late, first - late + block))
                blocks.append((ks[:reach], vs[:reach], q[first : first + block], u[first : first + block], bias))
        side = left[:late]
        q_late = jnp.concatenate([jnp.where(side, q[:late], 0), jnp.where(side, 0, q[:late])], 0).astype(bf16)
        u_late = jnp.concatenate([jnp.where(side, u[:late], 0), jnp.where(side, 0, u[:late])], 0).astype(bf16)
        blocks.append((k, v, q_late, u_late, (total, slice(rows, rows + 2 * late))))
        found = []

        def begin(i):
            ks, vs, qs, us, (reach, columns) = blocks[i]
            return products(ks, vs, qs, us, bias_ref[:reach, columns])

        ready = begin(0)
        for i, (ks, _, qs, us, _) in enumerate(blocks):
            now = ready
            if i + 1 < len(blocks):
                ready = begin(i + 1)
            rounded, ds = softmax_grads(*now)
            found.append((dims(rounded, us, 1, 0), dims(ds, qs, 1, 0), dims(ks, ds, 0, 0)))
        ends = found.pop()
        (v00, k00, q00), (v01, k01, q01), (v10, k10, q10), (v11, k11, q11) = found
        for n, (a0, a1, b0, b1, end) in enumerate(((k00, k01, k10, k11, ends[1]), (v00, v01, v10, v11, ends[0]))):
            both = jnp.where(left, a1, b1) + end
            g_ref[n, :low, span] = (both[:low] + jnp.where(left[:low], a0, b0)).astype(bf16)
            g_ref[n, low:, span] = both[low:].astype(bf16)
        dq_ref[span, :block] = ((q00 + q10) * factor).astype(bf16)
        dq_ref[span, block:rows] = ((q01 + q11) * factor).astype(bf16)
        upper = iota((128, late), 0) < HDIM
        dq_ref[span, rows:] = (jnp.where(upper, ends[2][:, :late], ends[2][:, late:]) * factor).astype(bf16)
        return carry

    for p in range(half // 128):
        pair(p, 0)

    def partial_of(lines):
        rest = dims(g_ref[0], weights_ref[1, lines, :], 1, 1) + dims(g_ref[1], weights_ref[2, lines, :], 1, 1)
        main = dims(dq_ref[:, :rows], weights_ref[0, lines, :], 0, 1)
        ends = dims(dq_ref[:, rows:], weights_ref[0, lines, :], 0, 1)
        return (rest + jnp.concatenate([ends, main], 0)).astype(bf16)

    first = jnp.zeros((total, 1), f32)
    second = jnp.zeros((total, 1), f32)
    for lines, ref, normed in ((own_rows, keep_ref, own), (other_rows, send_ref, peer)):
        part = partial_of(lines)
        ref[:, :half] = part
        part = part.astype(f32)
        mine = (lines is own_rows) == (head == 0)
        gain = jnp.where(mine, gain_ref[:, :half], gain_ref[:, half:])
        first = first + jnp.sum(part * gain, -1, keepdims=True)
        second = second + jnp.sum(part * normed.astype(f32), -1, keepdims=True)
    lane = iota((total, 128), 1)
    stats_ref[...] = jnp.where(lane == 0, first, jnp.where(lane == 1, second, 0.0))
    split = jnp.zeros((total, 128), f32)
    for n, value in enumerate(thirds(first) + thirds(second)):
        split = jnp.where(lane == n, value, split)
    send_ref[:, half:] = split.astype(bf16)


def combine_kernel(head_ref, keep_ref, got_ref, own_ref, stats_ref, gain_ref, out_ref):
    total, half = keep_ref.shape
    rows = out_ref.shape[0]
    late = total - rows
    width = 2 * half
    head = head_ref[0]
    own = own_ref[...].astype(f32)
    gain = jnp.where(head == 0, gain_ref[:, :half], gain_ref[:, half:])
    split, stats = got_ref[:, half:].astype(f32), stats_ref[...]
    first = (stats[:, 0:1] + (split[:, 0:1] + split[:, 1:2] + split[:, 2:3])) / width
    second = (stats[:, 1:2] + (split[:, 3:4] + split[:, 4:5] + split[:, 5:6])) / width
    inverse = 1.0 / gain
    grad = keep_ref[...].astype(f32) + got_ref[:, :half].astype(f32)
    gain_sum = jnp.sum(grad * own, 0, keepdims=True) * inverse
    result = (grad * gain - first - own * inverse * second).astype(bf16)
    out_ref[:, :half] = result[late:]
    ext = jnp.zeros((rows, 128), f32)
    put_row, put_col = iota((rows, late), 0), iota((rows, late), 1)
    piece = iota((rows, 128), 0) & 7
    for i in range(4):
        span = slice(i * 128, (i + 1) * 128)
        put = (put_row == put_col * 8 + i).astype(bf16)
        ext = ext + dims(put, result[:late, span], 1, 0)
        ext = jnp.where(piece == i + 4, gain_sum[:, span], ext)
    out_ref[:, half:] = ext.astype(bf16)


def finish_kernel(slots, back_ref, labrow_ref, spread_ref, out_ref, gain_ref):
    tokens, half = out_ref.shape
    rows = back_ref.shape[0]
    labrow = labrow_ref[...]
    lab = column_of(labrow)
    before = (lab == labrow) & (iota((tokens, tokens), 1) < iota((tokens, tokens), 0))
    rank = jnp.sum(before.astype(f32), -1, keepdims=True).astype(jnp.int32)
    key = jnp.where(rank < slots - 1, lab * 8 + rank, -1)
    last = jnp.where(rank == slots - 1, lab, -1)
    col = iota((tokens, rows), 1)
    hot = (col == key).astype(bf16)
    hot_last = jnp.where((col >> 3) == last, col & 7, -1)
    spread = spread_ref[...]
    ext = back_ref[:, half:]
    piece = iota((rows, 128), 0) & 7
    for i in range(half // 128):
        span = slice(i * 128, (i + 1) * 128)
        value = dims(hot, back_ref[:, span], 1, 0)
        value = value + dims((hot_last == i).astype(bf16), ext, 1, 0)
        out_ref[:, span] = (value * spread).astype(bf16)
        gain_ref[:, span] = jnp.sum(jnp.where(piece == i + 4, ext.astype(f32), 0.0), 0, keepdims=True)


def attend_call(head, recv, peer, projection, gain):
    rows, half = recv.shape[0], projection.shape[2]
    total = rows + rows // 8
    shape = jax.ShapeDtypeStruct
    return vmem_call(
        attend_kernel,
        (
            shape((total, half), bf16),
            shape((total, half + 128), bf16),
            shape((total, half), bf16),
            shape((total, 128), f32),
        ),
        scratch=[
            pltpu.VMEM((total, half), bf16),
            pltpu.VMEM((total, half), bf16),
            pltpu.VMEM((total, half), bf16),
            pltpu.VMEM((total, half), bf16),
            pltpu.VMEM((total, half), bf16),
            pltpu.VMEM((2, total, half), bf16),
            pltpu.VMEM((half, total), bf16),
            pltpu.VMEM((total, rows + 2 * (total - rows)), f32),
        ],
        limit=26,
        scalars=1,
        count=4,
    )(head, recv, peer, projection, gain)


def on_device(hidden, norm_gain, projection, upstream, cluster):
    sources = lax.axis_size("seq")
    tokens, width = hidden.shape[1:]
    half = projection.shape[2]
    slots = 3 * tokens // sources
    total, rows = sources * slots, sources * 8
    head = lax.axis_index("head").astype(jnp.int32).reshape(1)
    gain = norm_gain.reshape(1, width)
    labrow = cluster.reshape(1, tokens)
    shape = jax.ShapeDtypeStruct
    swap = [(0, 1), (1, 0)]

    sent, spread = vmem_call(
        lambda *refs: pack_kernel(slots, *refs),
        (shape((rows, width + 128), bf16), shape((tokens, 1), f32)),
        scalars=1,
        count=4,
    )(head, hidden[0], gain, upstream[0], labrow)
    recv = lax.all_to_all(sent.reshape(sources, 8, width + 128), "seq", 0, 0, tiled=True)
    recv = recv.reshape(rows, width + 128)
    peer = lax.ppermute(recv, "head", swap)
    keep, send, own, stats = attend_call(head, recv, peer, projection, gain)
    got = lax.ppermute(send, "head", swap)
    answer = vmem_call(combine_kernel, shape((rows, half + 128), bf16), scalars=1, count=5)(
        head, keep, got, own, stats, gain
    )
    back = lax.all_to_all(answer.reshape(sources, 8, half + 128), "seq", 0, 0, tiled=True)
    back = back.reshape(rows, half + 128)
    result, gain_sum = vmem_call(
        lambda *refs: finish_kernel(slots, *refs),
        (shape((tokens, half), bf16), shape((1, half), f32)),
        count=3,
    )(back, labrow, spread)
    gain_gradient = lax.psum(gain_sum.reshape(half), "dp") * (sources * lax.axis_size("dp") * tokens) ** (-0.5)
    return (result.reshape(1, tokens, half), gain_gradient)


def solution(mesh):
    in_specs = (
        P("dp", "seq", None),
        P(),
        P(None, None, "head"),
        P("dp", "seq", "head"),
        P("dp", "seq", None),
    )
    out_specs = (P("dp", "seq", "head"), P("head"))
    return jax.shard_map(
        on_device, mesh=mesh, in_specs=in_specs, out_specs=out_specs, check_vma=False
    )
```

```python
import jax
import jax.numpy as jnp
from jax import lax
from jax.experimental import pallas as pl
from jax.experimental.pallas import tpu as pltpu
from jax.sharding import PartitionSpec as P

HDIM = 64
EPSILON = 1e-05
MASKED = -1e30
PAD_MARK = 64.0
f32 = jnp.float32
bf16 = jnp.bfloat16


def dims(lhs, rhs, left, right):
    return lax.dot_general(lhs, rhs, (((left,), (right,)), ((), ())), preferred_element_type=f32)


def iota(shape, dim):
    return lax.broadcasted_iota(jnp.int32, shape, dim)


def vmem_call(kernel, out_shape, scratch=(), limit=8, scalars=0, count=1, space=None):
    spec = pl.BlockSpec(memory_space=pltpu.VMEM)
    source = spec if space is None else pl.BlockSpec(memory_space=space)
    return pl.pallas_call(
        kernel,
        out_shape=out_shape,
        in_specs=[pl.BlockSpec(memory_space=pltpu.SMEM)] * scalars + [source] * count,
        out_specs=jax.tree.map(lambda _: spec, out_shape),
        scratch_shapes=scratch,
        compiler_params=pltpu.CompilerParams(vmem_limit_bytes=limit * 2**20),
    )


def column_of(labels):
    count = labels.shape[1]
    same = iota((count, count), 0) == iota((count, count), 1)
    return jnp.sum(jnp.where(same, labels.astype(f32), 0.0), -1, keepdims=True).astype(jnp.int32)


def pack_kernel(slots, head_ref, hidden_any, gain_any, up_any, labrow_any, weights_any,
                out_ref, spread_ref, gain_ref, labrow_ref, weights_ref, hidden_ref, up_ref, sems):
    copies = [
        pltpu.make_async_copy(source, target, sems.at[n])
        for n, (source, target) in enumerate(
            (
                (labrow_any, labrow_ref),
                (gain_any, gain_ref),
                (hidden_any, hidden_ref),
                (up_any, up_ref),
                (weights_any, weights_ref),
            )
        )
    ]
    for copy in copies:
        copy.start()
    for copy in copies[:3]:
        copy.wait()
    tokens, width = hidden_ref.shape
    half = width // 2
    x = hidden_ref[...].astype(f32)
    center = x - jnp.mean(x, -1, keepdims=True)
    spread = lax.rsqrt(jnp.mean(center * center, -1, keepdims=True) + EPSILON)
    spread_ref[...] = spread
    normed = (center * spread * gain_ref[...]).astype(bf16)
    own = jnp.where(head_ref[0] == 0, normed[:, :half], normed[:, half:])
    copies[3].wait()
    up = up_ref[...]
    labrow = labrow_ref[...]
    lab = column_of(labrow)
    before = (lab == labrow) & (iota((tokens, tokens), 0) < iota((tokens, tokens), 1))
    rank = jnp.sum(before.astype(f32), 0, keepdims=True).astype(jnp.int32)
    rows = out_ref.shape[0]
    key = jnp.where(rank < slots - 1, labrow * 8 + rank, -1)
    last = jnp.where(rank == slots - 1, labrow, -1)
    row = iota((rows, tokens), 0)
    hot = (row == key).astype(f32)
    taken = jnp.sum(hot, -1, keepdims=True)
    hot = hot.astype(bf16)
    out_ref[:, :half] = dims(hot, own, 1, 0).astype(bf16)
    right = dims(hot, up, 1, 0)
    first = iota((rows, half), 1) == 0
    out_ref[:, half:width] = jnp.where(first & (taken == 0), PAD_MARK, right).astype(bf16)
    hot_last = ((row >> 3) == last).astype(f32)
    taken = jnp.sum(hot_last, -1, keepdims=True)
    piece = iota((rows, tokens), 0) & 7
    total = jnp.zeros((rows, 128), f32)
    for i in range(8):
        source = (own if i < 4 else up)[:, (i % 4) * 128 : (i % 4 + 1) * 128]
        total = total + dims(jnp.where(piece == i, hot_last, 0.0).astype(bf16), source, 1, 0)
    mark = (iota((rows, 128), 1) == 0) & ((iota((rows, 128), 0) & 7) == 4) & (taken == 0)
    out_ref[:, width:] = jnp.where(mark, PAD_MARK, total).astype(bf16)
    copies[4].wait()


def thirds(value):
    high = value.astype(bf16)
    rest = value - high.astype(f32)
    middle = rest.astype(bf16)
    return high.astype(f32), middle.astype(f32), rest - middle.astype(f32)


def attend_kernel(head_ref, recv_ref, other_ref, weights_ref, gain_ref, keep_ref, send_ref, own_ref, stats_ref,
                  peer_ref, u_ref, q_ref, k_ref, v_ref, g_ref, dq_ref, bias_ref):
    rows, extended = recv_ref.shape
    half = weights_ref.shape[2]
    width = 2 * half
    late = rows // 8
    total = rows + late
    head = head_ref[0]
    pick_col, pick_row = iota((late, rows), 1), iota((late, rows), 0)
    own_ref[late:, :] = recv_ref[:, :half]
    peer_ref[late:, :] = other_ref[:, :half]
    u_ref[late:, :] = recv_ref[:, half:width]
    for i in range(4):
        span = slice(i * 128, (i + 1) * 128)
        pick = (pick_col == pick_row * 8 + i).astype(bf16)
        own_ref[:late, span] = dims(pick, recv_ref[:, width:], 1, 0).astype(bf16)
        peer_ref[:late, span] = dims(pick, other_ref[:, width:], 1, 0).astype(bf16)
        pick = (pick_col == pick_row * 8 + (i + 4)).astype(bf16)
        u_ref[:late, span] = dims(pick, recv_ref[:, width:], 1, 0).astype(bf16)
    up = u_ref[:, :128].astype(f32)
    pads = up[:, :1] > 0.5 * PAD_MARK
    u_ref[:, :128] = jnp.where(pads & (iota((total, 128), 1) == 0), 0.0, up).astype(bf16)
    own_rows = pl.ds(pl.multiple_of(head * half, half), half)
    other_rows = pl.ds(pl.multiple_of((1 - head) * half, half), half)
    own, peer = own_ref[...], peer_ref[...]
    factor = HDIM**-0.5
    for n, ref in enumerate((q_ref, k_ref, v_ref)):
        made = dims(own, weights_ref[n, own_rows, :], 1, 0) + dims(peer, weights_ref[n, other_rows, :], 1, 0)
        ref[...] = (made * factor if n == 0 else made).astype(bf16)

    def order(i):
        return jnp.where(i < late, i * 9 + 8, ((i - late) >> 3) * 9 + ((i - late) & 7))

    place = jnp.where(pads, 2 * total, order(iota((total, 1), 0)))
    column = iota((1, rows), 1) + late
    bias_ref[:, :rows] = jnp.where(place <= order(column), 0.0, MASKED)
    column = iota((1, 2 * late), 1) & (late - 1)
    bias_ref[:, rows:] = jnp.where(place <= order(column), 0.0, MASKED)
    left = iota((total, 2 * HDIM), 1) < HDIM
    block = rows // 2
    low = late + block

    def products(k, v, q, u, bias):
        return dims(k, q, 1, 1) + bias, dims(v, u, 1, 1)

    def softmax_grads(scores, grads):
        powers = jnp.exp(scores - jnp.max(scores, 0, keepdims=True))
        weights = powers * (1.0 / jnp.sum(powers, 0, keepdims=True))
        rounded = weights.astype(bf16)
        center = jnp.sum(rounded.astype(f32) * grads, 0, keepdims=True)
        return rounded, (weights * (grads - center)).astype(bf16)

    def pair(p, carry):
        start = p * 128 if isinstance(p, int) else pl.multiple_of(p * 128, 128)
        span = pl.ds(start, 128)
        q, k, v, u = q_ref[:, span], k_ref[:, span], v_ref[:, span], u_ref[:, span]
        blocks = []
        for side in (left, ~left):
            ks = jnp.where(side, k, 0).astype(bf16)
            vs = jnp.where(side, v, 0).astype(bf16)
            for reach, first in ((low, late), (total, low)):
                bias = (reach, slice(first - late, first - late + block))
                blocks.append((ks[:reach], vs[:reach], q[first : first + block], u[first : first + block], bias))
        side = left[:late]
        q_late = jnp.concatenate([jnp.where(side, q[:late], 0), jnp.where(side, 0, q[:late])], 0).astype(bf16)
        u_late = jnp.concatenate([jnp.where(side, u[:late], 0), jnp.where(side, 0, u[:late])], 0).astype(bf16)
        blocks.append((k, v, q_late, u_late, (total, slice(rows, rows + 2 * late))))
        found = []

        def begin(i):
            ks, vs, qs, us, (reach, columns) = blocks[i]
            return products(ks, vs, qs, us, bias_ref[:reach, columns])

        ready = begin(0)
        for i, (ks, _, qs, us, _) in enumerate(blocks):
            now = ready
            if i + 1 < len(blocks):
                ready = begin(i + 1)
            rounded, ds = softmax_grads(*now)
            found.append((dims(rounded, us, 1, 0), dims(ds, qs, 1, 0), dims(ks, ds, 0, 0)))
        ends = found.pop()
        (v00, k00, q00), (v01, k01, q01), (v10, k10, q10), (v11, k11, q11) = found
        for n, (a0, a1, b0, b1, end) in enumerate(((k00, k01, k10, k11, ends[1]), (v00, v01, v10, v11, ends[0]))):
            both = jnp.where(left, a1, b1) + end
            g_ref[n, :low, span] = (both[:low] + jnp.where(left[:low], a0, b0)).astype(bf16)
            g_ref[n, low:, span] = both[low:].astype(bf16)
        dq_ref[span, :block] = ((q00 + q10) * factor).astype(bf16)
        dq_ref[span, block:rows] = ((q01 + q11) * factor).astype(bf16)
        upper = iota((128, late), 0) < HDIM
        dq_ref[span, rows:] = (jnp.where(upper, ends[2][:, :late], ends[2][:, late:]) * factor).astype(bf16)
        return carry

    for p in range(half // 128):
        pair(p, 0)

    def partial_of(lines):
        rest = dims(g_ref[0], weights_ref[1, lines, :], 1, 1) + dims(g_ref[1], weights_ref[2, lines, :], 1, 1)
        main = dims(dq_ref[:, :rows], weights_ref[0, lines, :], 0, 1)
        ends = dims(dq_ref[:, rows:], weights_ref[0, lines, :], 0, 1)
        return (rest + jnp.concatenate([ends, main], 0)).astype(bf16)

    first = jnp.zeros((total, 1), f32)
    second = jnp.zeros((total, 1), f32)
    for lines, ref, normed in ((own_rows, keep_ref, own), (other_rows, send_ref, peer)):
        part = partial_of(lines)
        ref[:, :half] = part
        part = part.astype(f32)
        mine = (lines is own_rows) == (head == 0)
        gain = jnp.where(mine, gain_ref[:, :half], gain_ref[:, half:])
        first = first + jnp.sum(part * gain, -1, keepdims=True)
        second = second + jnp.sum(part * normed.astype(f32), -1, keepdims=True)
    lane = iota((total, 128), 1)
    stats_ref[...] = jnp.where(lane == 0, first, jnp.where(lane == 1, second, 0.0))
    split = jnp.zeros((total, 128), f32)
    for n, value in enumerate(thirds(first) + thirds(second)):
        split = jnp.where(lane == n, value, split)
    send_ref[:, half:] = split.astype(bf16)


def combine_kernel(head_ref, keep_ref, got_ref, own_ref, stats_ref, gain_ref, out_ref):
    total, half = keep_ref.shape
    rows = out_ref.shape[0]
    late = total - rows
    width = 2 * half
    head = head_ref[0]
    own = own_ref[...].astype(f32)
    gain = jnp.where(head == 0, gain_ref[:, :half], gain_ref[:, half:])
    split, stats = got_ref[:, half:].astype(f32), stats_ref[...]
    first = (stats[:, 0:1] + (split[:, 0:1] + split[:, 1:2] + split[:, 2:3])) / width
    second = (stats[:, 1:2] + (split[:, 3:4] + split[:, 4:5] + split[:, 5:6])) / width
    inverse = 1.0 / gain
    grad = keep_ref[...].astype(f32) + got_ref[:, :half].astype(f32)
    gain_sum = jnp.sum(grad * own, 0, keepdims=True) * inverse
    result = (grad * gain - first - own * inverse * second).astype(bf16)
    out_ref[:, :half] = result[late:]
    ext = jnp.zeros((rows, 128), f32)
    put_row, put_col = iota((rows, late), 0), iota((rows, late), 1)
    piece = iota((rows, 128), 0) & 7
    for i in range(4):
        span = slice(i * 128, (i + 1) * 128)
        put = (put_row == put_col * 8 + i).astype(bf16)
        ext = ext + dims(put, result[:late, span], 1, 0)
        ext = jnp.where(piece == i + 4, gain_sum[:, span], ext)
    out_ref[:, half:] = ext.astype(bf16)


def finish_kernel(slots, scale, back_ref, labrow_ref, spread_ref, out_ref, gain_ref):
    tokens, half = out_ref.shape
    rows = back_ref.shape[0]
    labrow = labrow_ref[...]
    lab = column_of(labrow)
    before = (lab == labrow) & (iota((tokens, tokens), 1) < iota((tokens, tokens), 0))
    rank = jnp.sum(before.astype(f32), -1, keepdims=True).astype(jnp.int32)
    key = jnp.where(rank < slots - 1, lab * 8 + rank, -1)
    last = jnp.where(rank == slots - 1, lab, -1)
    col = iota((tokens, rows), 1)
    hot = (col == key).astype(bf16)
    hot_last = jnp.where((col >> 3) == last, col & 7, -1)
    spread = spread_ref[...]
    ext = back_ref[:, half:]
    piece = iota((rows, 128), 0) & 7
    for i in range(half // 128):
        span = slice(i * 128, (i + 1) * 128)
        value = dims(hot, back_ref[:, span], 1, 0)
        value = value + dims((hot_last == i).astype(bf16), ext, 1, 0)
        out_ref[:, span] = (value * spread).astype(bf16)
        gain_ref[:, span] = scale * jnp.sum(jnp.where(piece == i + 4, ext.astype(f32), 0.0), 0, keepdims=True)


def attend_call(head, recv, peer, projection, gain):
    rows, half = recv.shape[0], projection.shape[2]
    total = rows + rows // 8
    shape = jax.ShapeDtypeStruct
    return vmem_call(
        attend_kernel,
        (
            shape((total, half), bf16),
            shape((total, half + 128), bf16),
            shape((total, half), bf16),
            shape((total, 128), f32),
        ),
        scratch=[
            pltpu.VMEM((total, half), bf16),
            pltpu.VMEM((total, half), bf16),
            pltpu.VMEM((total, half), bf16),
            pltpu.VMEM((total, half), bf16),
            pltpu.VMEM((total, half), bf16),
            pltpu.VMEM((2, total, half), bf16),
            pltpu.VMEM((half, total), bf16),
            pltpu.VMEM((total, rows + 2 * (total - rows)), f32),
        ],
        limit=26,
        scalars=1,
        count=4,
    )(head, recv, peer, projection, gain)


def on_device(hidden, norm_gain, projection, upstream, cluster):
    sources = lax.axis_size("seq")
    tokens, width = hidden.shape[1:]
    half = projection.shape[2]
    slots = 3 * tokens // sources
    total, rows = sources * slots, sources * 8
    head = lax.axis_index("head").astype(jnp.int32).reshape(1)
    shape = jax.ShapeDtypeStruct
    swap = [(0, 1), (1, 0)]
    scale = (sources * lax.axis_size("dp") * tokens) ** (-0.5)

    sent, spread, gain, labrow, weights = vmem_call(
        lambda *refs: pack_kernel(slots, *refs),
        (
            shape((rows, width + 128), bf16),
            shape((tokens, 1), f32),
            shape((1, width), f32),
            shape((1, tokens), jnp.int32),
            shape(projection.shape, bf16),
        ),
        scratch=[
            pltpu.VMEM((tokens, width), bf16),
            pltpu.VMEM((tokens, half), bf16),
            pltpu.SemaphoreType.DMA((5,)),
        ],
        limit=12,
        scalars=1,
        count=5,
        space=pltpu.HBM,
    )(head, *[pltpu.with_memory_space_constraint(v, pltpu.HBM) for v in (hidden[0], norm_gain.reshape(1, width), upstream[0], cluster.reshape(1, tokens), projection)])
    recv = lax.all_to_all(sent.reshape(sources, 8, width + 128), "seq", 0, 0, tiled=True)
    recv = recv.reshape(rows, width + 128)
    peer = lax.ppermute(recv, "head", swap)
    keep, send, own, stats = attend_call(head, recv, peer, weights, gain)
    got = lax.ppermute(send, "head", swap)
    answer = vmem_call(combine_kernel, shape((rows, half + 128), bf16), scalars=1, count=5)(
        head, keep, got, own, stats, gain
    )
    back = lax.all_to_all(answer.reshape(sources, 8, half + 128), "seq", 0, 0, tiled=True)
    back = back.reshape(rows, half + 128)
    result, gain_sum = vmem_call(
        lambda *refs: finish_kernel(slots, scale, *refs),
        (shape((tokens, half), bf16), shape((1, half), f32)),
        count=3,
    )(back, labrow, spread)
    gain_gradient = lax.psum(gain_sum.reshape(half), "dp")
    return (result.reshape(1, tokens, half), gain_gradient)


def solution(mesh):
    in_specs = (
        P("dp", "seq", None),
        P(),
        P(None, None, "head"),
        P("dp", "seq", "head"),
        P("dp", "seq", None),
    )
    out_specs = (P("dp", "seq", "head"), P("head"))
    return jax.shard_map(
        on_device, mesh=mesh, in_specs=in_specs, out_specs=out_specs, check_vma=False
    )
```

```python
import jax
import jax.numpy as jnp
from jax import lax
from jax.experimental import pallas as pl
from jax.experimental.pallas import tpu as pltpu
from jax.sharding import PartitionSpec as P

HDIM = 64
EPSILON = 1e-05
MASKED = -1e30
PAD_MARK = 64.0
f32 = jnp.float32
bf16 = jnp.bfloat16


def dims(lhs, rhs, left, right):
    return lax.dot_general(lhs, rhs, (((left,), (right,)), ((), ())), preferred_element_type=f32)


def iota(shape, dim):
    return lax.broadcasted_iota(jnp.int32, shape, dim)


def vmem_call(kernel, out_shape, scratch=(), limit=8, scalars=0, count=1, space=pltpu.VMEM, cost=None):
    spec = pl.BlockSpec(memory_space=pltpu.VMEM)
    spaces = space if isinstance(space, tuple) else (space,) * count
    return pl.pallas_call(
        kernel,
        out_shape=out_shape,
        in_specs=[pl.BlockSpec(memory_space=pltpu.SMEM)] * scalars + [pl.BlockSpec(memory_space=m) for m in spaces],
        out_specs=jax.tree.map(lambda _: spec, out_shape),
        scratch_shapes=scratch,
        compiler_params=pltpu.CompilerParams(vmem_limit_bytes=limit * 2**20),
        cost_estimate=cost and pl.CostEstimate(flops=0, bytes_accessed=cost, transcendentals=0),
    )


def column_of(labels):
    count = labels.shape[1]
    same = iota((count, count), 0) == iota((count, count), 1)
    return jnp.sum(jnp.where(same, labels.astype(f32), 0.0), -1, keepdims=True).astype(jnp.int32)


def pack_kernel(slots, head_ref, hidden_any, gain_any, up_any, labrow_any,
                out_ref, spread_ref, gain_ref, labrow_ref, hidden_ref, up_ref, sems):
    copies = [
        pltpu.make_async_copy(source, target, sems.at[n])
        for n, (source, target) in enumerate(
            (
                (labrow_any, labrow_ref),
                (up_any, up_ref),
                (hidden_any, hidden_ref),
                (gain_any, gain_ref),
            )
        )
    ]
    for copy in copies:
        copy.start()
    copies[0].wait()
    tokens, width = hidden_ref.shape
    half = width // 2
    rows = out_ref.shape[0]
    labrow = labrow_ref[...]
    lab = column_of(labrow)
    before = (lab == labrow) & (iota((tokens, tokens), 0) < iota((tokens, tokens), 1))
    rank = jnp.sum(before.astype(f32), 0, keepdims=True).astype(jnp.int32)
    key = jnp.where(rank < slots - 1, labrow * 8 + rank, -1)
    last = jnp.where(rank == slots - 1, labrow, -1)
    row = iota((rows, tokens), 0)
    hot = (row == key).astype(f32)
    empty = jnp.sum(hot, -1, keepdims=True) == 0
    hot = hot.astype(bf16)
    hot_last = (row >> 3) == last
    empty_last = jnp.sum(hot_last.astype(f32), -1, keepdims=True) == 0
    pieces = [(hot_last & ((row & 7) == i)).astype(bf16) for i in range(8)]
    copies[1].wait()
    up = up_ref[...]
    right = dims(hot, up, 1, 0)
    first = iota((rows, half), 1) == 0
    out_ref[:, half:width] = jnp.where(first & empty, PAD_MARK, right).astype(bf16)
    total = jnp.zeros((rows, 128), f32)
    for i in range(4):
        total = total + dims(pieces[i + 4], up[:, i * 128 : (i + 1) * 128], 1, 0)
    copies[2].wait()
    copies[3].wait()
    x = hidden_ref[...].astype(f32)
    center = x - jnp.mean(x, -1, keepdims=True)
    spread = lax.rsqrt(jnp.mean(center * center, -1, keepdims=True) + EPSILON)
    spread_ref[...] = spread
    normed = (center * spread * gain_ref[...]).astype(bf16)
    own = jnp.where(head_ref[0] == 0, normed[:, :half], normed[:, half:])
    out_ref[:, :half] = dims(hot, own, 1, 0).astype(bf16)
    for i in range(4):
        total = total + dims(pieces[i], own[:, i * 128 : (i + 1) * 128], 1, 0)
    mark = (iota((rows, 128), 1) == 0) & ((iota((rows, 128), 0) & 7) == 4) & empty_last
    out_ref[:, width:] = jnp.where(mark, PAD_MARK, total).astype(bf16)


def thirds(value):
    high = value.astype(bf16)
    rest = value - high.astype(f32)
    middle = rest.astype(bf16)
    return high.astype(f32), middle.astype(f32), rest - middle.astype(f32)


def own_kernel(head_ref, recv_ref, weights_ref, own_ref, u_ref, bias_ref, acc_ref):
    rows = recv_ref.shape[0]
    half = weights_ref.shape[2]
    width = 2 * half
    late = rows // 8
    total = rows + late
    pick_col, pick_row = iota((late, rows), 1), iota((late, rows), 0)
    own_ref[late:, :] = recv_ref[:, :half]
    u_ref[late:, :] = recv_ref[:, half:width]
    for i in range(4):
        span = slice(i * 128, (i + 1) * 128)
        pick = (pick_col == pick_row * 8 + i).astype(bf16)
        own_ref[:late, span] = dims(pick, recv_ref[:, width:], 1, 0).astype(bf16)
        pick = (pick_col == pick_row * 8 + (i + 4)).astype(bf16)
        u_ref[:late, span] = dims(pick, recv_ref[:, width:], 1, 0).astype(bf16)
    up = u_ref[:, :128].astype(f32)
    pads = up[:, :1] > 0.5 * PAD_MARK
    u_ref[:, :128] = jnp.where(pads & (iota((total, 128), 1) == 0), 0.0, up).astype(bf16)
    own_rows = pl.ds(pl.multiple_of(head_ref[0] * half, half), half)
    own = own_ref[...]
    for n in range(3):
        acc_ref[n] = dims(own, weights_ref[n, own_rows, :], 1, 0)

    def order(i):
        return jnp.where(i < late, i * 9 + 8, ((i - late) >> 3) * 9 + ((i - late) & 7))

    place = jnp.where(pads, 2 * total, order(iota((total, 1), 0)))
    column = iota((1, rows), 1) + late
    bias_ref[:, :rows] = jnp.where(place <= order(column), 0.0, MASKED)
    column = iota((1, 2 * late), 1) & (late - 1)
    bias_ref[:, rows:] = jnp.where(place <= order(column), 0.0, MASKED)


def attend_kernel(head_ref, other_ref, own_ref, u_ref, bias_ref, acc_ref, weights_ref, gain_ref,
                  keep_ref, send_ref, stats_ref, peer_ref, q_ref, k_ref, v_ref, g_ref, dq_ref):
    rows = other_ref.shape[0]
    half = weights_ref.shape[2]
    width = 2 * half
    late = rows // 8
    total = rows + late
    head = head_ref[0]
    pick_col, pick_row = iota((late, rows), 1), iota((late, rows), 0)
    peer_ref[late:, :] = other_ref[:, :half]
    for i in range(4):
        pick = (pick_col == pick_row * 8 + i).astype(bf16)
        peer_ref[:late, i * 128 : (i + 1) * 128] = dims(pick, other_ref[:, width:], 1, 0).astype(bf16)
    own_rows = pl.ds(pl.multiple_of(head * half, half), half)
    other_rows = pl.ds(pl.multiple_of((1 - head) * half, half), half)
    own, peer = own_ref[...], peer_ref[...]
    factor = HDIM**-0.5
    for n, ref in enumerate((q_ref, k_ref, v_ref)):
        made = acc_ref[n] + dims(peer, weights_ref[n, other_rows, :], 1, 0)
        ref[...] = (made * factor if n == 0 else made).astype(bf16)

    left = iota((total, 2 * HDIM), 1) < HDIM
    block = rows // 2
    low = late + block

    def products(k, v, q, u, bias):
        return dims(k, q, 1, 1) + bias, dims(v, u, 1, 1)

    def softmax_grads(scores, grads):
        powers = jnp.exp(scores - jnp.max(scores, 0, keepdims=True))
        weights = powers * (1.0 / jnp.sum(powers, 0, keepdims=True))
        rounded = weights.astype(bf16)
        center = jnp.sum(rounded.astype(f32) * grads, 0, keepdims=True)
        return rounded, (weights * (grads - center)).astype(bf16)

    def pair(p, carry):
        start = p * 128 if isinstance(p, int) else pl.multiple_of(p * 128, 128)
        span = pl.ds(start, 128)
        q, k, v, u = q_ref[:, span], k_ref[:, span], v_ref[:, span], u_ref[:, span]
        blocks = []
        for side in (left, ~left):
            ks = jnp.where(side, k, 0).astype(bf16)
            vs = jnp.where(side, v, 0).astype(bf16)
            for reach, first in ((low, late), (total, low)):
                bias = (reach, slice(first - late, first - late + block))
                blocks.append((ks[:reach], vs[:reach], q[first : first + block], u[first : first + block], bias))
        side = left[:late]
        q_late = jnp.concatenate([jnp.where(side, q[:late], 0), jnp.where(side, 0, q[:late])], 0).astype(bf16)
        u_late = jnp.concatenate([jnp.where(side, u[:late], 0), jnp.where(side, 0, u[:late])], 0).astype(bf16)
        blocks.append((k, v, q_late, u_late, (total, slice(rows, rows + 2 * late))))
        found = []

        def begin(i):
            ks, vs, qs, us, (reach, columns) = blocks[i]
            return products(ks, vs, qs, us, bias_ref[:reach, columns])

        ready = begin(0)
        for i, (ks, _, qs, us, _) in enumerate(blocks):
            now = ready
            if i + 1 < len(blocks):
                ready = begin(i + 1)
            rounded, ds = softmax_grads(*now)
            found.append((dims(rounded, us, 1, 0), dims(ds, qs, 1, 0), dims(ks, ds, 0, 0)))
        ends = found.pop()
        (v00, k00, q00), (v01, k01, q01), (v10, k10, q10), (v11, k11, q11) = found
        for n, (a0, a1, b0, b1, end) in enumerate(((k00, k01, k10, k11, ends[1]), (v00, v01, v10, v11, ends[0]))):
            both = jnp.where(left, a1, b1) + end
            g_ref[n, :low, span] = (both[:low] + jnp.where(left[:low], a0, b0)).astype(bf16)
            g_ref[n, low:, span] = both[low:].astype(bf16)
        dq_ref[span, :block] = ((q00 + q10) * factor).astype(bf16)
        dq_ref[span, block:rows] = ((q01 + q11) * factor).astype(bf16)
        upper = iota((128, late), 0) < HDIM
        dq_ref[span, rows:] = (jnp.where(upper, ends[2][:, :late], ends[2][:, late:]) * factor).astype(bf16)
        return carry

    for p in range(half // 128):
        pair(p, 0)

    def partial_of(lines):
        rest = dims(g_ref[0], weights_ref[1, lines, :], 1, 1) + dims(g_ref[1], weights_ref[2, lines, :], 1, 1)
        main = dims(dq_ref[:, :rows], weights_ref[0, lines, :], 0, 1)
        ends = dims(dq_ref[:, rows:], weights_ref[0, lines, :], 0, 1)
        return (rest + jnp.concatenate([ends, main], 0)).astype(bf16)

    first = jnp.zeros((total, 1), f32)
    second = jnp.zeros((total, 1), f32)
    for lines, ref, normed in ((own_rows, keep_ref, own), (other_rows, send_ref, peer)):
        part = partial_of(lines)
        ref[:, :half] = part
        part = part.astype(f32)
        mine = (lines is own_rows) == (head == 0)
        gain = jnp.where(mine, gain_ref[:, :half], gain_ref[:, half:])
        first = first + jnp.sum(part * gain, -1, keepdims=True)
        second = second + jnp.sum(part * normed.astype(f32), -1, keepdims=True)
    lane = iota((total, 128), 1)
    stats_ref[...] = jnp.where(lane == 0, first, jnp.where(lane == 1, second, 0.0))
    split = jnp.zeros((total, 128), f32)
    for n, value in enumerate(thirds(first) + thirds(second)):
        split = jnp.where(lane == n, value, split)
    send_ref[:, half:] = split.astype(bf16)


def combine_kernel(head_ref, keep_ref, got_ref, own_ref, stats_ref, gain_ref, out_ref):
    total, half = keep_ref.shape
    rows = out_ref.shape[0]
    late = total - rows
    width = 2 * half
    head = head_ref[0]
    own = own_ref[...].astype(f32)
    gain = jnp.where(head == 0, gain_ref[:, :half], gain_ref[:, half:])
    split, stats = got_ref[:, half:].astype(f32), stats_ref[...]
    first = (stats[:, 0:1] + (split[:, 0:1] + split[:, 1:2] + split[:, 2:3])) / width
    second = (stats[:, 1:2] + (split[:, 3:4] + split[:, 4:5] + split[:, 5:6])) / width
    inverse = 1.0 / gain
    grad = keep_ref[...].astype(f32) + got_ref[:, :half].astype(f32)
    gain_sum = jnp.sum(grad * own, 0, keepdims=True) * inverse
    result = (grad * gain - first - own * inverse * second).astype(bf16)
    out_ref[:, :half] = result[late:]
    ext = jnp.zeros((rows, 128), f32)
    put_row, put_col = iota((rows, late), 0), iota((rows, late), 1)
    piece = iota((rows, 128), 0) & 7
    for i in range(4):
        span = slice(i * 128, (i + 1) * 128)
        put = (put_row == put_col * 8 + i).astype(bf16)
        ext = ext + dims(put, result[:late, span], 1, 0)
        ext = jnp.where(piece == i + 4, gain_sum[:, span], ext)
    out_ref[:, half:] = ext.astype(bf16)


def prepare_kernel(slots, weights_any, labrow_ref, weights_ref, hot_ref, sem):
    copy = pltpu.make_async_copy(weights_any, weights_ref, sem)
    copy.start()
    tokens, rows = hot_ref.shape[1:]
    labrow = labrow_ref[...]
    lab = column_of(labrow)
    before = (lab == labrow) & (iota((tokens, tokens), 1) < iota((tokens, tokens), 0))
    rank = jnp.sum(before.astype(f32), -1, keepdims=True).astype(jnp.int32)
    key = jnp.where(rank < slots - 1, lab * 8 + rank, -1)
    last = jnp.where(rank == slots - 1, lab, -1)
    col = iota((tokens, rows), 1)
    hot_last = jnp.where((col >> 3) == last, col & 7, -1)
    hot_ref[4] = (col == key).astype(bf16)
    for i in range(4):
        hot_ref[i] = (hot_last == i).astype(bf16)
    copy.wait()


def finish_kernel(scale, back_ref, hot_ref, spread_ref, out_ref, gain_ref):
    half = out_ref.shape[1]
    rows = back_ref.shape[0]
    spread = spread_ref[...]
    ext = back_ref[:, half:]
    piece = iota((rows, 128), 0) & 7
    for i in range(half // 128):
        span = slice(i * 128, (i + 1) * 128)
        value = dims(hot_ref[4], back_ref[:, span], 1, 0) + dims(hot_ref[i], ext, 1, 0)
        out_ref[:, span] = (value * spread).astype(bf16)
        gain_ref[:, span] = scale * jnp.sum(jnp.where(piece == i + 4, ext.astype(f32), 0.0), 0, keepdims=True)


def own_call(head, recv, projection):
    rows, half = recv.shape[0], projection.shape[2]
    total = rows + rows // 8
    shape = jax.ShapeDtypeStruct
    return vmem_call(
        own_kernel,
        (
            shape((total, half), bf16),
            shape((total, half), bf16),
            shape((total, rows + 2 * (total - rows)), f32),
            shape((3, total, half), f32),
        ),
        limit=20,
        cost=6 * 10**6,
        scalars=1,
        count=2,
    )(head, recv, projection)


def attend_call(head, peer, own, up, bias, acc, projection, gain):
    rows, half = peer.shape[0], projection.shape[2]
    total = rows + rows // 8
    shape = jax.ShapeDtypeStruct
    return vmem_call(
        attend_kernel,
        (shape((total, half), bf16), shape((total, half + 128), bf16), shape((total, 128), f32)),
        scratch=[
            pltpu.VMEM((total, half), bf16),
            pltpu.VMEM((total, half), bf16),
            pltpu.VMEM((total, half), bf16),
            pltpu.VMEM((total, half), bf16),
            pltpu.VMEM((2, total, half), bf16),
            pltpu.VMEM((half, total), bf16),
        ],
        limit=26,
        scalars=1,
        count=7,
    )(head, peer, own, up, bias, acc, projection, gain)


def in_hbm(array):
    return pltpu.with_memory_space_constraint(array, pltpu.HBM)


def on_device(hidden, norm_gain, projection, upstream, cluster):
    sources = lax.axis_size("seq")
    tokens, width = hidden.shape[1:]
    half = projection.shape[2]
    slots = 3 * tokens // sources
    total, rows = sources * slots, sources * 8
    head = lax.axis_index("head").astype(jnp.int32).reshape(1)
    shape = jax.ShapeDtypeStruct
    swap = [(0, 1), (1, 0)]
    scale = (sources * lax.axis_size("dp") * tokens) ** (-0.5)

    sent, spread, gain, labrow = vmem_call(
        lambda *refs: pack_kernel(slots, *refs),
        (
            shape((rows, width + 128), bf16),
            shape((tokens, 1), f32),
            shape((1, width), f32),
            shape((1, tokens), jnp.int32),
        ),
        scratch=[
            pltpu.VMEM((tokens, width), bf16),
            pltpu.VMEM((tokens, half), bf16),
            pltpu.SemaphoreType.DMA((4,)),
        ],
        scalars=1,
        count=4,
        space=pltpu.HBM,
    )(head, *[in_hbm(v) for v in (hidden[0], norm_gain.reshape(1, width), upstream[0], cluster.reshape(1, tokens))])
    weights, hots = vmem_call(
        lambda *refs: prepare_kernel(slots, *refs),
        (shape(projection.shape, bf16), shape((5, tokens, rows), bf16)),
        scratch=[pltpu.SemaphoreType.DMA(())],
        cost=6 * 10**6,
        scalars=0,
        count=2,
        space=(pltpu.HBM, pltpu.VMEM),
    )(in_hbm(projection), labrow)
    recv = lax.all_to_all(sent.reshape(sources, 8, width + 128), "seq", 0, 0, tiled=True)
    recv, weights, hots = lax.optimization_barrier((recv.reshape(rows, width + 128), weights, hots))
    peer = lax.ppermute(recv, "head", swap)
    own, up, bias, acc = own_call(head, recv, weights)
    keep, send, stats = attend_call(head, peer, own, up, bias, acc, weights, gain)
    got = lax.ppermute(send, "head", swap)
    answer = vmem_call(combine_kernel, shape((rows, half + 128), bf16), scalars=1, count=5)(
        head, keep, got, own, stats, gain
    )
    back = lax.all_to_all(answer.reshape(sources, 8, half + 128), "seq", 0, 0, tiled=True)
    back = back.reshape(rows, half + 128)
    result, gain_sum = vmem_call(
        lambda *refs: finish_kernel(scale, *refs),
        (shape((tokens, half), bf16), shape((1, half), f32)),
        count=3,
    )(back, hots, spread)
    gain_gradient = lax.psum(gain_sum.reshape(half), "dp")
    return (result.reshape(1, tokens, half), gain_gradient)


def solution(mesh):
    in_specs = (
        P("dp", "seq", None),
        P(),
        P(None, None, "head"),
        P("dp", "seq", "head"),
        P("dp", "seq", None),
    )
    out_specs = (P("dp", "seq", "head"), P("head"))
    return jax.shard_map(
        on_device, mesh=mesh, in_specs=in_specs, out_specs=out_specs, check_vma=False
    )
```

```python
import jax
import jax.numpy as jnp
from jax import lax
from jax.experimental import pallas as pl
from jax.experimental.pallas import tpu as pltpu
from jax.sharding import PartitionSpec as P

HDIM = 64
EPSILON = 1e-05
MASKED = -1e30
PAD_MARK = 64.0
f32 = jnp.float32
bf16 = jnp.bfloat16


def dims(lhs, rhs, left, right):
    return lax.dot_general(lhs, rhs, (((left,), (right,)), ((), ())), preferred_element_type=f32)


def iota(shape, dim):
    return lax.broadcasted_iota(jnp.int32, shape, dim)


def vmem_call(kernel, out_shape, scratch=(), limit=8, scalars=0, count=1, space=pltpu.VMEM, cost=None):
    spec = pl.BlockSpec(memory_space=pltpu.VMEM)
    spaces = space if isinstance(space, tuple) else (space,) * count
    return pl.pallas_call(
        kernel,
        out_shape=out_shape,
        in_specs=[pl.BlockSpec(memory_space=pltpu.SMEM)] * scalars + [pl.BlockSpec(memory_space=m) for m in spaces],
        out_specs=jax.tree.map(lambda _: spec, out_shape),
        scratch_shapes=scratch,
        compiler_params=pltpu.CompilerParams(vmem_limit_bytes=limit * 2**20),
        cost_estimate=cost and pl.CostEstimate(flops=0, bytes_accessed=cost, transcendentals=0),
    )


def column_of(labels):
    count = labels.shape[1]
    same = iota((count, count), 0) == iota((count, count), 1)
    return jnp.sum(jnp.where(same, labels.astype(f32), 0.0), -1, keepdims=True).astype(jnp.int32)


def pack_kernel(slots, head_ref, hidden_any, gain_any, up_any, labrow_any, weights_any,
                out_ref, spread_ref, gain_ref, labrow_ref, weights_ref, hidden_ref, up_ref, sems):
    copies = [
        pltpu.make_async_copy(source, target, sems.at[n])
        for n, (source, target) in enumerate(
            (
                (labrow_any, labrow_ref),
                (gain_any, gain_ref),
                (hidden_any, hidden_ref),
                (up_any, up_ref),
                (weights_any, weights_ref),
            )
        )
    ]
    for copy in copies:
        copy.start()
    for copy in copies[:3]:
        copy.wait()
    tokens, width = hidden_ref.shape
    half = width // 2
    x = hidden_ref[...].astype(f32)
    center = x - jnp.mean(x, -1, keepdims=True)
    spread = lax.rsqrt(jnp.mean(center * center, -1, keepdims=True) + EPSILON)
    spread_ref[...] = spread
    normed = (center * spread * gain_ref[...]).astype(bf16)
    own = jnp.where(head_ref[0] == 0, normed[:, :half], normed[:, half:])
    copies[3].wait()
    up = up_ref[...]
    labrow = labrow_ref[...]
    lab = column_of(labrow)
    before = (lab == labrow) & (iota((tokens, tokens), 0) < iota((tokens, tokens), 1))
    rank = jnp.sum(before.astype(f32), 0, keepdims=True).astype(jnp.int32)
    rows = out_ref.shape[0]
    key = jnp.where(rank < slots - 1, labrow * 8 + rank, -1)
    last = jnp.where(rank == slots - 1, labrow, -1)
    row = iota((rows, tokens), 0)
    hot = (row == key).astype(f32)
    taken = jnp.sum(hot, -1, keepdims=True)
    hot = hot.astype(bf16)
    out_ref[:, :half] = dims(hot, own, 1, 0).astype(bf16)
    right = dims(hot, up, 1, 0)
    first = iota((rows, half), 1) == 0
    out_ref[:, half:width] = jnp.where(first & (taken == 0), PAD_MARK, right).astype(bf16)
    hot_last = ((row >> 3) == last).astype(f32)
    taken = jnp.sum(hot_last, -1, keepdims=True)
    piece = iota((rows, tokens), 0) & 7
    total = jnp.zeros((rows, 128), f32)
    for i in range(8):
        source = (own if i < 4 else up)[:, (i % 4) * 128 : (i % 4 + 1) * 128]
        total = total + dims(jnp.where(piece == i, hot_last, 0.0).astype(bf16), source, 1, 0)
    mark = (iota((rows, 128), 1) == 0) & ((iota((rows, 128), 0) & 7) == 4) & (taken == 0)
    out_ref[:, width:] = jnp.where(mark, PAD_MARK, total).astype(bf16)
    copies[4].wait()


def thirds(value):
    high = value.astype(bf16)
    rest = value - high.astype(f32)
    middle = rest.astype(bf16)
    return high.astype(f32), middle.astype(f32), rest - middle.astype(f32)


def own_kernel(slots, head_ref, recv_ref, weights_ref, labrow_ref, own_ref, u_ref, bias_ref, acc_ref, hot_ref):
    rows = recv_ref.shape[0]
    half = weights_ref.shape[2]
    width = 2 * half
    late = rows // 8
    total = rows + late
    pick_col, pick_row = iota((late, rows), 1), iota((late, rows), 0)
    own_ref[late:, :] = recv_ref[:, :half]
    u_ref[late:, :] = recv_ref[:, half:width]
    for i in range(4):
        span = slice(i * 128, (i + 1) * 128)
        pick = (pick_col == pick_row * 8 + i).astype(bf16)
        own_ref[:late, span] = dims(pick, recv_ref[:, width:], 1, 0).astype(bf16)
        pick = (pick_col == pick_row * 8 + (i + 4)).astype(bf16)
        u_ref[:late, span] = dims(pick, recv_ref[:, width:], 1, 0).astype(bf16)
    up = u_ref[:, :128].astype(f32)
    pads = up[:, :1] > 0.5 * PAD_MARK
    u_ref[:, :128] = jnp.where(pads & (iota((total, 128), 1) == 0), 0.0, up).astype(bf16)
    own_rows = pl.ds(pl.multiple_of(head_ref[0] * half, half), half)
    own = own_ref[...]
    for n in range(3):
        acc_ref[n] = dims(own, weights_ref[n, own_rows, :], 1, 0)

    def order(i):
        return jnp.where(i < late, i * 9 + 8, ((i - late) >> 3) * 9 + ((i - late) & 7))

    place = jnp.where(pads, 2 * total, order(iota((total, 1), 0)))
    column = iota((1, rows), 1) + late
    bias_ref[:, :rows] = jnp.where(place <= order(column), 0.0, MASKED)
    column = iota((1, 2 * late), 1) & (late - 1)
    bias_ref[:, rows:] = jnp.where(place <= order(column), 0.0, MASKED)
    tokens = hot_ref.shape[1]
    labrow = labrow_ref[...]
    lab = column_of(labrow)
    before = (lab == labrow) & (iota((tokens, tokens), 1) < iota((tokens, tokens), 0))
    rank = jnp.sum(before.astype(f32), -1, keepdims=True).astype(jnp.int32)
    key = jnp.where(rank < slots - 1, lab * 8 + rank, -1)
    last = jnp.where(rank == slots - 1, lab, -1)
    col = iota((tokens, rows), 1)
    hot_last = jnp.where((col >> 3) == last, col & 7, -1)
    hot_ref[4] = (col == key).astype(bf16)
    for i in range(4):
        hot_ref[i] = (hot_last == i).astype(bf16)


def attend_kernel(head_ref, other_ref, own_ref, u_ref, bias_ref, acc_ref, weights_ref, gain_ref,
                  keep_ref, send_ref, stats_ref, peer_ref, q_ref, k_ref, v_ref, g_ref, dq_ref):
    rows = other_ref.shape[0]
    half = weights_ref.shape[2]
    width = 2 * half
    late = rows // 8
    total = rows + late
    head = head_ref[0]
    pick_col, pick_row = iota((late, rows), 1), iota((late, rows), 0)
    peer_ref[late:, :] = other_ref[:, :half]
    for i in range(4):
        pick = (pick_col == pick_row * 8 + i).astype(bf16)
        peer_ref[:late, i * 128 : (i + 1) * 128] = dims(pick, other_ref[:, width:], 1, 0).astype(bf16)
    own_rows = pl.ds(pl.multiple_of(head * half, half), half)
    other_rows = pl.ds(pl.multiple_of((1 - head) * half, half), half)
    own, peer = own_ref[...], peer_ref[...]
    factor = HDIM**-0.5
    for n, ref in enumerate((q_ref, k_ref, v_ref)):
        made = acc_ref[n] + dims(peer, weights_ref[n, other_rows, :], 1, 0)
        ref[...] = (made * factor if n == 0 else made).astype(bf16)

    left = iota((total, 2 * HDIM), 1) < HDIM
    block = rows // 2
    low = late + block

    def products(k, v, q, u, bias):
        return dims(k, q, 1, 1) + bias, dims(v, u, 1, 1)

    def softmax_grads(scores, grads):
        powers = jnp.exp(scores - jnp.max(scores, 0, keepdims=True))
        weights = powers * (1.0 / jnp.sum(powers, 0, keepdims=True))
        rounded = weights.astype(bf16)
        center = jnp.sum(rounded.astype(f32) * grads, 0, keepdims=True)
        return rounded, (weights * (grads - center)).astype(bf16)

    def pair(p, carry):
        start = p * 128 if isinstance(p, int) else pl.multiple_of(p * 128, 128)
        span = pl.ds(start, 128)
        q, k, v, u = q_ref[:, span], k_ref[:, span], v_ref[:, span], u_ref[:, span]
        blocks = []
        for side in (left, ~left):
            ks = jnp.where(side, k, 0).astype(bf16)
            vs = jnp.where(side, v, 0).astype(bf16)
            for reach, first in ((low, late), (total, low)):
                bias = (reach, slice(first - late, first - late + block))
                blocks.append((ks[:reach], vs[:reach], q[first : first + block], u[first : first + block], bias))
        side = left[:late]
        q_late = jnp.concatenate([jnp.where(side, q[:late], 0), jnp.where(side, 0, q[:late])], 0).astype(bf16)
        u_late = jnp.concatenate([jnp.where(side, u[:late], 0), jnp.where(side, 0, u[:late])], 0).astype(bf16)
        blocks.append((k, v, q_late, u_late, (total, slice(rows, rows + 2 * late))))
        found = []

        def begin(i):
            ks, vs, qs, us, (reach, columns) = blocks[i]
            return products(ks, vs, qs, us, bias_ref[:reach, columns])

        ready = begin(0)
        for i, (ks, _, qs, us, _) in enumerate(blocks):
            now = ready
            if i + 1 < len(blocks):
                ready = begin(i + 1)
            rounded, ds = softmax_grads(*now)
            found.append((dims(rounded, us, 1, 0), dims(ds, qs, 1, 0), dims(ks, ds, 0, 0)))
        ends = found.pop()
        (v00, k00, q00), (v01, k01, q01), (v10, k10, q10), (v11, k11, q11) = found
        for n, (a0, a1, b0, b1, end) in enumerate(((k00, k01, k10, k11, ends[1]), (v00, v01, v10, v11, ends[0]))):
            both = jnp.where(left, a1, b1) + end
            g_ref[n, :low, span] = (both[:low] + jnp.where(left[:low], a0, b0)).astype(bf16)
            g_ref[n, low:, span] = both[low:].astype(bf16)
        dq_ref[span, :block] = ((q00 + q10) * factor).astype(bf16)
        dq_ref[span, block:rows] = ((q01 + q11) * factor).astype(bf16)
        upper = iota((128, late), 0) < HDIM
        dq_ref[span, rows:] = (jnp.where(upper, ends[2][:, :late], ends[2][:, late:]) * factor).astype(bf16)
        return carry

    for p in range(half // 128):
        pair(p, 0)

    def partial_of(lines):
        rest = dims(g_ref[0], weights_ref[1, lines, :], 1, 1) + dims(g_ref[1], weights_ref[2, lines, :], 1, 1)
        main = dims(dq_ref[:, :rows], weights_ref[0, lines, :], 0, 1)
        ends = dims(dq_ref[:, rows:], weights_ref[0, lines, :], 0, 1)
        return (rest + jnp.concatenate([ends, main], 0)).astype(bf16)

    first = jnp.zeros((total, 1), f32)
    second = jnp.zeros((total, 1), f32)
    for lines, ref, normed in ((own_rows, keep_ref, own), (other_rows, send_ref, peer)):
        part = partial_of(lines)
        ref[:, :half] = part
        part = part.astype(f32)
        mine = (lines is own_rows) == (head == 0)
        gain = jnp.where(mine, gain_ref[:, :half], gain_ref[:, half:])
        first = first + jnp.sum(part * gain, -1, keepdims=True)
        second = second + jnp.sum(part * normed.astype(f32), -1, keepdims=True)
    lane = iota((total, 128), 1)
    stats_ref[...] = jnp.where(lane == 0, first, jnp.where(lane == 1, second, 0.0))
    split = jnp.zeros((total, 128), f32)
    for n, value in enumerate(thirds(first) + thirds(second)):
        split = jnp.where(lane == n, value, split)
    send_ref[:, half:] = split.astype(bf16)


def combine_kernel(head_ref, keep_ref, got_ref, own_ref, stats_ref, gain_ref, out_ref):
    total, half = keep_ref.shape
    rows = out_ref.shape[0]
    late = total - rows
    width = 2 * half
    head = head_ref[0]
    own = own_ref[...].astype(f32)
    gain = jnp.where(head == 0, gain_ref[:, :half], gain_ref[:, half:])
    split, stats = got_ref[:, half:].astype(f32), stats_ref[...]
    first = (stats[:, 0:1] + (split[:, 0:1] + split[:, 1:2] + split[:, 2:3])) / width
    second = (stats[:, 1:2] + (split[:, 3:4] + split[:, 4:5] + split[:, 5:6])) / width
    inverse = 1.0 / gain
    grad = keep_ref[...].astype(f32) + got_ref[:, :half].astype(f32)
    gain_sum = jnp.sum(grad * own, 0, keepdims=True) * inverse
    result = (grad * gain - first - own * inverse * second).astype(bf16)
    out_ref[:, :half] = result[late:]
    ext = jnp.zeros((rows, 128), f32)
    put_row, put_col = iota((rows, late), 0), iota((rows, late), 1)
    piece = iota((rows, 128), 0) & 7
    for i in range(4):
        span = slice(i * 128, (i + 1) * 128)
        put = (put_row == put_col * 8 + i).astype(bf16)
        ext = ext + dims(put, result[:late, span], 1, 0)
        ext = jnp.where(piece == i + 4, gain_sum[:, span], ext)
    out_ref[:, half:] = ext.astype(bf16)


def finish_kernel(scale, back_ref, hot_ref, spread_ref, out_ref, gain_ref):
    half = out_ref.shape[1]
    rows = back_ref.shape[0]
    spread = spread_ref[...]
    ext = back_ref[:, half:]
    piece = iota((rows, 128), 0) & 7
    for i in range(half // 128):
        span = slice(i * 128, (i + 1) * 128)
        value = dims(hot_ref[4], back_ref[:, span], 1, 0) + dims(hot_ref[i], ext, 1, 0)
        out_ref[:, span] = (value * spread).astype(bf16)
        gain_ref[:, span] = scale * jnp.sum(jnp.where(piece == i + 4, ext.astype(f32), 0.0), 0, keepdims=True)


def own_call(slots, head, recv, projection, labrow):
    rows, half = recv.shape[0], projection.shape[2]
    total = rows + rows // 8
    shape = jax.ShapeDtypeStruct
    return vmem_call(
        lambda *refs: own_kernel(slots, *refs),
        (
            shape((total, half), bf16),
            shape((total, half), bf16),
            shape((total, rows + 2 * (total - rows)), f32),
            shape((3, total, half), f32),
            shape((5, labrow.shape[1], rows), bf16),
        ),
        limit=20,
        cost=6 * 10**6,
        scalars=1,
        count=3,
    )(head, recv, projection, labrow)


def attend_call(head, peer, own, up, bias, acc, projection, gain):
    rows, half = peer.shape[0], projection.shape[2]
    total = rows + rows // 8
    shape = jax.ShapeDtypeStruct
    return vmem_call(
        attend_kernel,
        (shape((total, half), bf16), shape((total, half + 128), bf16), shape((total, 128), f32)),
        scratch=[
            pltpu.VMEM((total, half), bf16),
            pltpu.VMEM((total, half), bf16),
            pltpu.VMEM((total, half), bf16),
            pltpu.VMEM((total, half), bf16),
            pltpu.VMEM((2, total, half), bf16),
            pltpu.VMEM((half, total), bf16),
        ],
        limit=26,
        scalars=1,
        count=7,
    )(head, peer, own, up, bias, acc, projection, gain)


def on_device(hidden, norm_gain, projection, upstream, cluster):
    sources = lax.axis_size("seq")
    tokens, width = hidden.shape[1:]
    half = projection.shape[2]
    slots = 3 * tokens // sources
    total, rows = sources * slots, sources * 8
    head = lax.axis_index("head").astype(jnp.int32).reshape(1)
    shape = jax.ShapeDtypeStruct
    swap = [(0, 1), (1, 0)]
    scale = (sources * lax.axis_size("dp") * tokens) ** (-0.5)

    sent, spread, gain, labrow, weights = vmem_call(
        lambda *refs: pack_kernel(slots, *refs),
        (
            shape((rows, width + 128), bf16),
            shape((tokens, 1), f32),
            shape((1, width), f32),
            shape((1, tokens), jnp.int32),
            shape(projection.shape, bf16),
        ),
        scratch=[
            pltpu.VMEM((tokens, width), bf16),
            pltpu.VMEM((tokens, half), bf16),
            pltpu.SemaphoreType.DMA((5,)),
        ],
        limit=12,
        scalars=1,
        count=5,
        space=pltpu.HBM,
    )(head, *[pltpu.with_memory_space_constraint(v, pltpu.HBM) for v in (hidden[0], norm_gain.reshape(1, width), upstream[0], cluster.reshape(1, tokens), projection)])
    recv = lax.all_to_all(sent.reshape(sources, 8, width + 128), "seq", 0, 0, tiled=True)
    recv = recv.reshape(rows, width + 128)
    peer = lax.ppermute(recv, "head", swap)
    own, up, bias, acc, hots = own_call(slots, head, recv, weights, labrow)
    keep, send, stats = attend_call(head, peer, own, up, bias, acc, weights, gain)
    got = lax.ppermute(send, "head", swap)
    answer = vmem_call(combine_kernel, shape((rows, half + 128), bf16), scalars=1, count=5)(
        head, keep, got, own, stats, gain
    )
    back = lax.all_to_all(answer.reshape(sources, 8, half + 128), "seq", 0, 0, tiled=True)
    back = back.reshape(rows, half + 128)
    result, gain_sum = vmem_call(
        lambda *refs: finish_kernel(scale, *refs),
        (shape((tokens, half), bf16), shape((1, half), f32)),
        count=3,
    )(back, hots, spread)
    gain_gradient = lax.psum(gain_sum.reshape(half), "dp")
    return (result.reshape(1, tokens, half), gain_gradient)


def solution(mesh):
    in_specs = (
        P("dp", "seq", None),
        P(),
        P(None, None, "head"),
        P("dp", "seq", "head"),
        P("dp", "seq", None),
    )
    out_specs = (P("dp", "seq", "head"), P("head"))
    return jax.shard_map(
        on_device, mesh=mesh, in_specs=in_specs, out_specs=out_specs, check_vma=False
    )
```

```python
import jax
import jax.numpy as jnp
from jax import lax
from jax.experimental import pallas as pl
from jax.experimental.pallas import tpu as pltpu
from jax.sharding import PartitionSpec as P

HDIM = 64
EPSILON = 1e-05
MASKED = -1e30
PAD_MARK = 64.0
f32 = jnp.float32
bf16 = jnp.bfloat16


def dims(lhs, rhs, left, right):
    return lax.dot_general(lhs, rhs, (((left,), (right,)), ((), ())), preferred_element_type=f32)


def iota(shape, dim):
    return lax.broadcasted_iota(jnp.int32, shape, dim)


def vmem_call(kernel, out_shape, scratch=(), limit=8, scalars=0, count=1, space=pltpu.VMEM, cost=None):
    spec = pl.BlockSpec(memory_space=pltpu.VMEM)
    spaces = space if isinstance(space, tuple) else (space,) * count
    return pl.pallas_call(
        kernel,
        out_shape=out_shape,
        in_specs=[pl.BlockSpec(memory_space=pltpu.SMEM)] * scalars + [pl.BlockSpec(memory_space=m) for m in spaces],
        out_specs=jax.tree.map(lambda _: spec, out_shape),
        scratch_shapes=scratch,
        compiler_params=pltpu.CompilerParams(vmem_limit_bytes=limit * 2**20),
        cost_estimate=cost and pl.CostEstimate(flops=0, bytes_accessed=cost, transcendentals=0),
    )


def column_of(labels):
    count = labels.shape[1]
    same = iota((count, count), 0) == iota((count, count), 1)
    return jnp.sum(jnp.where(same, labels.astype(f32), 0.0), -1, keepdims=True).astype(jnp.int32)


def pack_kernel(slots, head_ref, hidden_any, gain_any, up_any, labrow_any, weights_any,
                out_ref, spread_ref, gain_ref, labrow_ref, weights_ref, hidden_ref, up_ref, sems):
    copies = [
        pltpu.make_async_copy(source, target, sems.at[n])
        for n, (source, target) in enumerate(
            (
                (labrow_any, labrow_ref),
                (gain_any, gain_ref),
                (hidden_any, hidden_ref),
                (up_any, up_ref),
                (weights_any, weights_ref),
            )
        )
    ]
    for copy in copies:
        copy.start()
    copies[0].wait()
    tokens, width = hidden_ref.shape
    half = width // 2
    rows = out_ref.shape[0]
    labrow = labrow_ref[...]
    lab = column_of(labrow)
    before = (lab == labrow) & (iota((tokens, tokens), 0) < iota((tokens, tokens), 1))
    rank = jnp.sum(before.astype(f32), 0, keepdims=True).astype(jnp.int32)
    key = jnp.where(rank < slots - 1, labrow * 8 + rank, -1)
    last = jnp.where(rank == slots - 1, labrow, -1)
    row = iota((rows, tokens), 0)
    hot = (row == key).astype(f32)
    taken = jnp.sum(hot, -1, keepdims=True)
    hot = hot.astype(bf16)
    for copy in copies[1:4]:
        copy.wait()
    x = hidden_ref[...].astype(f32)
    center = x - jnp.mean(x, -1, keepdims=True)
    spread = lax.rsqrt(jnp.mean(center * center, -1, keepdims=True) + EPSILON)
    spread_ref[...] = spread
    normed = (center * spread * gain_ref[...]).astype(bf16)
    own = jnp.where(head_ref[0] == 0, normed[:, :half], normed[:, half:])
    up = up_ref[...]
    out_ref[:, :half] = dims(hot, own, 1, 0).astype(bf16)
    right = dims(hot, up, 1, 0)
    first = iota((rows, half), 1) == 0
    out_ref[:, half:width] = jnp.where(first & (taken == 0), PAD_MARK, right).astype(bf16)
    hot_last = ((row >> 3) == last).astype(f32)
    taken = jnp.sum(hot_last, -1, keepdims=True)
    piece = iota((rows, tokens), 0) & 7
    total = jnp.zeros((rows, 128), f32)
    for i in range(8):
        source = (own if i < 4 else up)[:, (i % 4) * 128 : (i % 4 + 1) * 128]
        total = total + dims(jnp.where(piece == i, hot_last, 0.0).astype(bf16), source, 1, 0)
    mark = (iota((rows, 128), 1) == 0) & ((iota((rows, 128), 0) & 7) == 4) & (taken == 0)
    out_ref[:, width:] = jnp.where(mark, PAD_MARK, total).astype(bf16)
    copies[4].wait()


def thirds(value):
    high = value.astype(bf16)
    rest = value - high.astype(f32)
    middle = rest.astype(bf16)
    return high.astype(f32), middle.astype(f32), rest - middle.astype(f32)


def own_kernel(slots, head_ref, recv_ref, weights_ref, labrow_ref, own_ref, u_ref, bias_ref, acc_ref, hot_ref):
    rows = recv_ref.shape[0]
    half = weights_ref.shape[2]
    width = 2 * half
    late = rows // 8
    total = rows + late
    pick_col, pick_row = iota((late, rows), 1), iota((late, rows), 0)
    own_ref[late:, :] = recv_ref[:, :half]
    u_ref[late:, :] = recv_ref[:, half:width]
    for i in range(4):
        span = slice(i * 128, (i + 1) * 128)
        pick = (pick_col == pick_row * 8 + i).astype(bf16)
        own_ref[:late, span] = dims(pick, recv_ref[:, width:], 1, 0).astype(bf16)
        pick = (pick_col == pick_row * 8 + (i + 4)).astype(bf16)
        u_ref[:late, span] = dims(pick, recv_ref[:, width:], 1, 0).astype(bf16)
    up = u_ref[:, :128].astype(f32)
    pads = up[:, :1] > 0.5 * PAD_MARK
    u_ref[:, :128] = jnp.where(pads & (iota((total, 128), 1) == 0), 0.0, up).astype(bf16)
    own_rows = pl.ds(pl.multiple_of(head_ref[0] * half, half), half)
    own = own_ref[...]
    for n in range(3):
        acc_ref[n] = dims(own, weights_ref[n, own_rows, :], 1, 0)

    def order(i):
        return jnp.where(i < late, i * 9 + 8, ((i - late) >> 3) * 9 + ((i - late) & 7))

    place = jnp.where(pads, 2 * total, order(iota((total, 1), 0)))
    column = iota((1, rows), 1) + late
    bias_ref[:, :rows] = jnp.where(place <= order(column), 0.0, MASKED)
    column = iota((1, 2 * late), 1) & (late - 1)
    bias_ref[:, rows:] = jnp.where(place <= order(column), 0.0, MASKED)
    tokens = hot_ref.shape[1]
    labrow = labrow_ref[...]
    lab = column_of(labrow)
    before = (lab == labrow) & (iota((tokens, tokens), 1) < iota((tokens, tokens), 0))
    rank = jnp.sum(before.astype(f32), -1, keepdims=True).astype(jnp.int32)
    key = jnp.where(rank < slots - 1, lab * 8 + rank, -1)
    last = jnp.where(rank == slots - 1, lab, -1)
    col = iota((tokens, rows), 1)
    hot_last = jnp.where((col >> 3) == last, col & 7, -1)
    hot_ref[4] = (col == key).astype(bf16)
    for i in range(4):
        hot_ref[i] = (hot_last == i).astype(bf16)


def attend_kernel(head_ref, other_ref, own_ref, u_ref, bias_ref, acc_ref, weights_ref, gain_ref,
                  keep_ref, send_ref, stats_ref, peer_ref, q_ref, k_ref, v_ref, g_ref, dq_ref):
    rows = other_ref.shape[0]
    half = weights_ref.shape[2]
    width = 2 * half
    late = rows // 8
    total = rows + late
    head = head_ref[0]
    pick_col, pick_row = iota((late, rows), 1), iota((late, rows), 0)
    peer_ref[late:, :] = other_ref[:, :half]
    for i in range(4):
        pick = (pick_col == pick_row * 8 + i).astype(bf16)
        peer_ref[:late, i * 128 : (i + 1) * 128] = dims(pick, other_ref[:, width:], 1, 0).astype(bf16)
    own_rows = pl.ds(pl.multiple_of(head * half, half), half)
    other_rows = pl.ds(pl.multiple_of((1 - head) * half, half), half)
    own, peer = own_ref[...], peer_ref[...]
    factor = HDIM**-0.5
    for n, ref in enumerate((q_ref, k_ref, v_ref)):
        made = acc_ref[n] + dims(peer, weights_ref[n, other_rows, :], 1, 0)
        ref[...] = (made * factor if n == 0 else made).astype(bf16)

    left = iota((total, 2 * HDIM), 1) < HDIM
    block = rows // 2
    low = late + block

    def products(k, v, q, u, bias):
        return dims(k, q, 1, 1) + bias, dims(v, u, 1, 1)

    def softmax_grads(scores, grads):
        powers = jnp.exp(scores - jnp.max(scores, 0, keepdims=True))
        weights = powers * (1.0 / jnp.sum(powers, 0, keepdims=True))
        rounded = weights.astype(bf16)
        center = jnp.sum(rounded.astype(f32) * grads, 0, keepdims=True)
        return rounded, (weights * (grads - center)).astype(bf16)

    def pair(p, carry):
        start = p * 128 if isinstance(p, int) else pl.multiple_of(p * 128, 128)
        span = pl.ds(start, 128)
        q, k, v, u = q_ref[:, span], k_ref[:, span], v_ref[:, span], u_ref[:, span]
        blocks = []
        for side in (left, ~left):
            ks = jnp.where(side, k, 0).astype(bf16)
            vs = jnp.where(side, v, 0).astype(bf16)
            for reach, first in ((low, late), (total, low)):
                bias = (reach, slice(first - late, first - late + block))
                blocks.append((ks[:reach], vs[:reach], q[first : first + block], u[first : first + block], bias))
        side = left[:late]
        q_late = jnp.concatenate([jnp.where(side, q[:late], 0), jnp.where(side, 0, q[:late])], 0).astype(bf16)
        u_late = jnp.concatenate([jnp.where(side, u[:late], 0), jnp.where(side, 0, u[:late])], 0).astype(bf16)
        blocks.append((k, v, q_late, u_late, (total, slice(rows, rows + 2 * late))))
        found = []

        def begin(i):
            ks, vs, qs, us, (reach, columns) = blocks[i]
            return products(ks, vs, qs, us, bias_ref[:reach, columns])

        ready = begin(0)
        for i, (ks, _, qs, us, _) in enumerate(blocks):
            now = ready
            if i + 1 < len(blocks):
                ready = begin(i + 1)
            rounded, ds = softmax_grads(*now)
            found.append((dims(rounded, us, 1, 0), dims(ds, qs, 1, 0), dims(ks, ds, 0, 0)))
        ends = found.pop()
        (v00, k00, q00), (v01, k01, q01), (v10, k10, q10), (v11, k11, q11) = found
        for n, (a0, a1, b0, b1, end) in enumerate(((k00, k01, k10, k11, ends[1]), (v00, v01, v10, v11, ends[0]))):
            both = jnp.where(left, a1, b1) + end
            g_ref[n, :low, span] = (both[:low] + jnp.where(left[:low], a0, b0)).astype(bf16)
            g_ref[n, low:, span] = both[low:].astype(bf16)
        dq_ref[span, :block] = ((q00 + q10) * factor).astype(bf16)
        dq_ref[span, block:rows] = ((q01 + q11) * factor).astype(bf16)
        upper = iota((128, late), 0) < HDIM
        dq_ref[span, rows:] = (jnp.where(upper, ends[2][:, :late], ends[2][:, late:]) * factor).astype(bf16)
        return carry

    for p in range(half // 128):
        pair(p, 0)

    def partial_of(lines):
        rest = dims(g_ref[0], weights_ref[1, lines, :], 1, 1) + dims(g_ref[1], weights_ref[2, lines, :], 1, 1)
        main = dims(dq_ref[:, :rows], weights_ref[0, lines, :], 0, 1)
        ends = dims(dq_ref[:, rows:], weights_ref[0, lines, :], 0, 1)
        return (rest + jnp.concatenate([ends, main], 0)).astype(bf16)

    first = jnp.zeros((total, 1), f32)
    second = jnp.zeros((total, 1), f32)
    for lines, ref, normed in ((own_rows, keep_ref, own), (other_rows, send_ref, peer)):
        part = partial_of(lines)
        ref[:, :half] = part
        part = part.astype(f32)
        mine = (lines is own_rows) == (head == 0)
        gain = jnp.where(mine, gain_ref[:, :half], gain_ref[:, half:])
        first = first + jnp.sum(part * gain, -1, keepdims=True)
        second = second + jnp.sum(part * normed.astype(f32), -1, keepdims=True)
    lane = iota((total, 128), 1)
    stats_ref[...] = jnp.where(lane == 0, first, jnp.where(lane == 1, second, 0.0))
    split = jnp.zeros((total, 128), f32)
    for n, value in enumerate(thirds(first) + thirds(second)):
        split = jnp.where(lane == n, value, split)
    send_ref[:, half:] = split.astype(bf16)


def combine_kernel(head_ref, keep_ref, got_ref, own_ref, stats_ref, gain_ref, out_ref):
    total, half = keep_ref.shape
    rows = out_ref.shape[0]
    late = total - rows
    width = 2 * half
    head = head_ref[0]
    own = own_ref[...].astype(f32)
    gain = jnp.where(head == 0, gain_ref[:, :half], gain_ref[:, half:])
    split, stats = got_ref[:, half:].astype(f32), stats_ref[...]
    first = (stats[:, 0:1] + (split[:, 0:1] + split[:, 1:2] + split[:, 2:3])) / width
    second = (stats[:, 1:2] + (split[:, 3:4] + split[:, 4:5] + split[:, 5:6])) / width
    inverse = 1.0 / gain
    grad = keep_ref[...].astype(f32) + got_ref[:, :half].astype(f32)
    gain_sum = jnp.sum(grad * own, 0, keepdims=True) * inverse
    result = (grad * gain - first - own * inverse * second).astype(bf16)
    out_ref[:, :half] = result[late:]
    ext = jnp.zeros((rows, 128), f32)
    put_row, put_col = iota((rows, late), 0), iota((rows, late), 1)
    piece = iota((rows, 128), 0) & 7
    for i in range(4):
        span = slice(i * 128, (i + 1) * 128)
        put = (put_row == put_col * 8 + i).astype(bf16)
        ext = ext + dims(put, result[:late, span], 1, 0)
        ext = jnp.where(piece == i + 4, gain_sum[:, span], ext)
    out_ref[:, half:] = ext.astype(bf16)


def finish_kernel(scale, back_ref, hot_ref, spread_ref, out_ref, gain_ref):
    half = out_ref.shape[1]
    rows = back_ref.shape[0]
    spread = spread_ref[...]
    ext = back_ref[:, half:]
    piece = iota((rows, 128), 0) & 7
    for i in range(half // 128):
        span = slice(i * 128, (i + 1) * 128)
        value = dims(hot_ref[4], back_ref[:, span], 1, 0) + dims(hot_ref[i], ext, 1, 0)
        out_ref[:, span] = (value * spread).astype(bf16)
        gain_ref[:, span] = scale * jnp.sum(jnp.where(piece == i + 4, ext.astype(f32), 0.0), 0, keepdims=True)


def own_call(slots, head, recv, projection, labrow):
    rows, half = recv.shape[0], projection.shape[2]
    total = rows + rows // 8
    shape = jax.ShapeDtypeStruct
    return vmem_call(
        lambda *refs: own_kernel(slots, *refs),
        (
            shape((total, half), bf16),
            shape((total, half), bf16),
            shape((total, rows + 2 * (total - rows)), f32),
            shape((3, total, half), f32),
            shape((5, labrow.shape[1], rows), bf16),
        ),
        limit=20,
        cost=6 * 10**6,
        scalars=1,
        count=3,
    )(head, recv, projection, labrow)


def attend_call(head, peer, own, up, bias, acc, projection, gain):
    rows, half = peer.shape[0], projection.shape[2]
    total = rows + rows // 8
    shape = jax.ShapeDtypeStruct
    return vmem_call(
        attend_kernel,
        (shape((total, half), bf16), shape((total, half + 128), bf16), shape((total, 128), f32)),
        scratch=[
            pltpu.VMEM((total, half), bf16),
            pltpu.VMEM((total, half), bf16),
            pltpu.VMEM((total, half), bf16),
            pltpu.VMEM((total, half), bf16),
            pltpu.VMEM((2, total, half), bf16),
            pltpu.VMEM((half, total), bf16),
        ],
        limit=26,
        scalars=1,
        count=7,
    )(head, peer, own, up, bias, acc, projection, gain)


def on_device(hidden, norm_gain, projection, upstream, cluster):
    sources = lax.axis_size("seq")
    tokens, width = hidden.shape[1:]
    half = projection.shape[2]
    slots = 3 * tokens // sources
    total, rows = sources * slots, sources * 8
    head = lax.axis_index("head").astype(jnp.int32).reshape(1)
    shape = jax.ShapeDtypeStruct
    swap = [(0, 1), (1, 0)]
    scale = (sources * lax.axis_size("dp") * tokens) ** (-0.5)

    sent, spread, gain, labrow, weights = vmem_call(
        lambda *refs: pack_kernel(slots, *refs),
        (
            shape((rows, width + 128), bf16),
            shape((tokens, 1), f32),
            shape((1, width), f32),
            shape((1, tokens), jnp.int32),
            shape(projection.shape, bf16),
        ),
        scratch=[
            pltpu.VMEM((tokens, width), bf16),
            pltpu.VMEM((tokens, half), bf16),
            pltpu.SemaphoreType.DMA((5,)),
        ],
        limit=12,
        scalars=1,
        count=5,
        space=pltpu.HBM,
    )(head, *[pltpu.with_memory_space_constraint(v, pltpu.HBM) for v in (hidden[0], norm_gain.reshape(1, width), upstream[0], cluster.reshape(1, tokens), projection)])
    recv = lax.all_to_all(sent.reshape(sources, 8, width + 128), "seq", 0, 0, tiled=True)
    recv = recv.reshape(rows, width + 128)
    peer = lax.ppermute(recv, "head", swap)
    own, up, bias, acc, hots = own_call(slots, head, recv, weights, labrow)
    keep, send, stats = attend_call(head, peer, own, up, bias, acc, weights, gain)
    got = lax.ppermute(send, "head", swap)
    answer = vmem_call(combine_kernel, shape((rows, half + 128), bf16), scalars=1, count=5)(
        head, keep, got, own, stats, gain
    )
    back = lax.all_to_all(answer.reshape(sources, 8, half + 128), "seq", 0, 0, tiled=True)
    back = back.reshape(rows, half + 128)
    result, gain_sum = vmem_call(
        lambda *refs: finish_kernel(scale, *refs),
        (shape((tokens, half), bf16), shape((1, half), f32)),
        count=3,
    )(back, hots, spread)
    gain_gradient = lax.psum(gain_sum.reshape(half), "dp")
    return (result.reshape(1, tokens, half), gain_gradient)


def solution(mesh):
    in_specs = (
        P("dp", "seq", None),
        P(),
        P(None, None, "head"),
        P("dp", "seq", "head"),
        P("dp", "seq", None),
    )
    out_specs = (P("dp", "seq", "head"), P("head"))
    return jax.shard_map(
        on_device, mesh=mesh, in_specs=in_specs, out_specs=out_specs, check_vma=False
    )
```
